256 devices in a mesh: facet: 16 (over y_lo, x, core), chan: 16 (over z, y_hi).
Axes of the slice: x: 4, y: 4 (y_hi: 2, y_lo: 2; y = y_hi * 2 + y_lo), z: 8, core: 2. Of those that a mesh axis runs over, the one named last changes fastest.
Arguments:
- sky_image: float32 [256, 512, 512], P('chan', 'facet')
- margins: int32 [16], replicated, may hold values from 1 to 7, as said below
- wavelet_dual: float32 [4, 256, 512, 512], P(None, 'chan', 'facet'), may hold values from -2.5 to 2.5
- sparsity_weights: float32 [4, 512, 512], P(None, 'facet'), may hold values from 0.25 to 4
- lowrank_dual: float32 [256, 512, 512], P(None, 'facet', 'chan'), may hold values from -6 to 6
- kernel_weights: bfloat16 [16, 32, 32, 512], P('chan'), may hold values from -0.25 to 0.25
- tile_index: int32 [16, 32], P('chan'), may hold values from 1 to 1023
- data_dual: float32 [256, 2, 1024], P(('chan', 'facet')), may hold values from -6 to 6
- visibilities: float32 [256, 2, 1024], P(('chan', 'facet')), may hold values from -6 to 6
- radius_scale: float32 [256], P(('chan', 'facet')), may hold values from 0.5 to 8
Outputs:
- wavelet_next: float32 [4, 256, 512, 512], P(None, 'chan', 'facet')
- lowrank_next: float32 [256, 512, 512], P(None, 'facet', 'chan')
- data_next: float32 [256, 2, 1024], P(('chan', 'facet'))
The draws below stay inside these ranges and needn't reach their ends.
Inputs may be any that keep to these rules, and one draw needn't show every extreme that they name: `margins`: some facet other than the first has margin 7.
All inputs are finite; a program needn't handle non-finite values.
Results may differ from the reference program's by a relative error of at most 0.0003.
Values sent between devices are 32-bit elements; how exact they have to be, the bound alone decides.
No kernel may reach another device: no remote copies, remote signals or barrier semaphores. Data moves between devices by JAX's collectives and lax.ppermute only.
A program may use at most 128 MiB of HBM per device.

```python
import math
import jax
import jax.numpy as jnp
from jax import lax

RF = 32
N = 512
NFAC = 16
CG = 16
GROUPS = 16
L = 256
SUB = 4
OV = 7
NSTEP = 5
KT = 16
NT = 1024
NBLK = 32
VB = 32
NVIS = 1024


def draw_sky_image(key, part):
    key = jax.random.fold_in(key, 11)
    amp_key, index_key, texture_key = jax.random.split(key, 3)
    frequency = jnp.linspace(-1.0, 1.0, L, dtype=jnp.float32)
    spectral = jax.random.uniform(index_key, (1, N, N), jnp.float32, -1.0, 1.0)
    amplitude = jnp.exp(jax.random.uniform(amp_key, (1, N, N), jnp.float32, math.log(0.05), math.log(3.0)))
    texture = jnp.exp(jax.random.uniform(texture_key, (L, N, N), jnp.float32, math.log(0.6), math.log(1.5)))
    return amplitude * jnp.exp((spectral - 0.55) * frequency[:, None, None]) * texture


def draw_margins(key, part):
    key = jax.random.fold_in(key, 23)
    width_key, place_key = jax.random.split(key)
    widths = jax.random.randint(width_key, (NFAC,), 1, OV + 1)
    widest = jax.random.randint(place_key, (), 1, NFAC)
    return widths.at[widest].set(OV)


def touch_ends(entries, own_key, least, high):
    longest = entries.shape.index(max(entries.shape))
    spots = []
    for shift in (0, 1):
        where = [jax.random.randint(jax.random.fold_in(own_key, axis), (), 0, length) for axis, length in enumerate(entries.shape)]
        where[longest] = (where[longest] + shift) % entries.shape[longest]
        spots.append(tuple(where))
    return entries.at[spots[0]].set(least).at[spots[1]].set(high)


def levels(stream_key, dims, cuts, low, top_value):
    level, own = 1.0, jax.random.fold_in(stream_key, 6)
    for position, parts in cuts:
        heights = jnp.exp(jax.random.uniform(jax.random.fold_in(own, position), (parts,), jnp.float32, low / len(cuts), top_value / len(cuts)))
        level = level * jnp.repeat(heights, dims[position] // parts).reshape([-1 if axis == position else 1 for axis in range(len(dims))])
    return level


def bell_draw(key, shape, scale, most, shards=(), kind=jnp.bfloat16):
    values = scale * jax.random.normal(key, shape, jnp.float32)
    if shards:
        values = values * levels(key, shape, shards, -0.22, 0.18)
    return jnp.clip(values, -most, most).astype(kind)


def setup_inputs(seed: int = 0) -> dict:
    keys = jax.random.split(jax.random.key(seed), 11)
    sky_image = draw_sky_image(jax.random.fold_in(keys[10], 71), 0)
    margins = draw_margins(jax.random.fold_in(keys[10], 71), 0)
    wavelet_dual = bell_draw(keys[2], (SUB, L, N, N), 0.3, 2.5, ((1, 16), (2, 16)), jnp.float32)
    sparsity_weights = jnp.clip(jnp.exp(math.log(4.0) - 2.7725887 * jax.random.uniform(keys[3], (SUB, N, N), jnp.float32) ** levels(keys[3], (SUB, N, N), ((1, 16),), -0.2, 0.2)), 0.25, 4.0)
    lowrank_dual = bell_draw(keys[4], (L, N, N), 1.0, 6.0, ((1, 16), (2, 16)), jnp.float32)
    kernel_weights = bell_draw(keys[5], (GROUPS, NBLK, VB, 2 * KT * KT), (2 * KT * KT) ** -0.5, 0.25, ((0, 16),))
    tile_index = touch_ends(jax.random.randint(keys[6], (GROUPS, NBLK), 1, NT), jax.random.fold_in(keys[6], 1), 1, NT - 1).astype(jnp.int32)
    data_dual = bell_draw(keys[7], (L, 2, NVIS), 1.0, 6.0, ((0, 256),), jnp.float32)
    visibilities = bell_draw(keys[8], (L, 2, NVIS), 1.0, 6.0, ((0, 256),), jnp.float32)
    radius_scale = jnp.clip(jnp.exp(math.log(8.0) - 2.7725887 * jax.random.uniform(keys[9], (L,), jnp.float32) ** levels(keys[9], (L,), ((0, 256),), -0.2, 0.2)), 0.5, 8.0)
    return {"sky_image": sky_image, "margins": margins, "wavelet_dual": wavelet_dual, "sparsity_weights": sparsity_weights, "lowrank_dual": lowrank_dual, "kernel_weights": kernel_weights, "tile_index": tile_index, "data_dual": data_dual, "visibilities": visibilities, "radius_scale": radius_scale}


highest = lax.Precision.HIGHEST
low_taps = (-0.010597401784997278, 0.032883011666982945, 0.030841381835986965, -0.18703481171888114, -0.02798376941698385, 0.6308807679295904, 0.7148465705525415, 0.23037781330885523)
high_taps = tuple(((-1.0) ** offset * low_taps[7 - offset] for offset in range(8)))

def causal_rows(values, filter_taps, lower):
    row_count = values.shape[1]
    positions = jnp.arange(row_count, dtype=jnp.int32)
    summed = filter_taps[0] * values
    for offset in range(1, 8):
        shifted = jnp.pad(values, ((0, 0), (offset, 0), (0, 0)))[:, :row_count, :]
        kept_rows = (positions - offset >= lower).astype(values.dtype)
        summed = summed + filter_taps[offset] * shifted * kept_rows[None, :, None]
    return summed

def column_pass(values, filter_taps):
    col_count = values.shape[-1]
    padded = jnp.pad(values, ((0, 0), (0, 0), (7, 0)))
    summed = filter_taps[0] * values
    for offset in range(1, 8):
        summed = summed + filter_taps[offset] * padded[:, :, 7 - offset:7 - offset + col_count]
    return summed

def inverse_root(gram, pixel_count):
    size_now = gram.shape[0]
    identity = jnp.eye(size_now, dtype=gram.dtype)
    shifted = identity + gram / pixel_count
    frobenius = jnp.sqrt(jnp.sum(shifted * shifted))
    current = shifted / frobenius
    inverse = identity
    for turn in range(NSTEP):
        middle = 1.5 * identity - 0.5 * jnp.dot(inverse, current, precision=highest)
        current = jnp.dot(current, middle, precision=highest)
        inverse = jnp.dot(middle, inverse, precision=highest)
    return inverse / jnp.sqrt(frobenius)

def degrid(real_part, imag_part, kernel_block, tile_ids):
    chan_count = real_part.shape[0]
    image_side = real_part.shape[1]
    tiles_side = image_side // KT

    def to_tiles(values):
        shaped = values.reshape(chan_count, tiles_side, KT, tiles_side, KT).transpose(0, 1, 3, 2, 4)
        return shaped.reshape(chan_count, tiles_side * tiles_side, KT * KT)[:, tile_ids, :]
    picked_real = to_tiles(real_part)
    picked_imag = to_tiles(imag_part)
    stacked = jnp.stack([jnp.concatenate([picked_real, -picked_imag], axis=-1), jnp.concatenate([picked_imag, picked_real], axis=-1)], axis=1)
    predicted = jnp.einsum('bvk,ncbk->ncbv', kernel_block.astype(jnp.float32), stacked, precision=highest)
    return predicted.reshape(chan_count, 2, -1)

def data_step(data_dual, forward, visibilities, radius_scale):
    moved = data_dual + forward
    residual = 2.0 * moved - visibilities
    distance = jnp.sqrt(lax.optimization_barrier(jnp.sum(residual * residual, axis=(1, 2))) + 1e-06)
    radius = radius_scale * math.sqrt(2.0 * visibilities.shape[2])
    shrink = jnp.minimum(1.0, radius / distance)
    return moved - 0.5 * (visibilities + residual * shrink[:, None, None])

def reference(sky_image, margins, wavelet_dual, sparsity_weights, lowrank_dual, kernel_weights, tile_index, data_dual, visibilities, radius_scale):
    row_ids = jnp.arange(N, dtype=jnp.int32)
    facet_ids = row_ids // RF
    lower = facet_ids * RF - margins[facet_ids]
    low_rows = causal_rows(sky_image, low_taps, lower)
    high_rows = causal_rows(sky_image, high_taps, lower)
    pairs = ((low_rows, low_taps), (low_rows, high_taps), (high_rows, low_taps), (high_rows, high_taps))
    updated = []
    for number, (filtered, column_taps) in enumerate(pairs):
        blended = wavelet_dual[number] + 0.5 * column_pass(filtered, column_taps)
        energy = lax.optimization_barrier(jnp.sum(blended * blended, axis=0))
        factor = jnp.maximum(1.0, jnp.sqrt(energy / L) / sparsity_weights[number])
        updated.append(blended / factor[None])
    wavelet_next = jnp.stack(updated)
    blended_r = lowrank_dual + 0.5 * sky_image
    stacked = blended_r.reshape(L, NFAC, RF * N).transpose(1, 0, 2)

    def one_facet(block):
        gram = jnp.dot(block, block.T, precision=highest, preferred_element_type=jnp.float32)
        mixer = inverse_root(gram, RF * N)
        return jnp.dot(mixer, block, precision=highest, preferred_element_type=jnp.float32)
    lowrank_next = lax.map(one_facet, stacked).transpose(1, 0, 2).reshape(L, N, N)
    spectrum = jnp.fft.fft2(sky_image) / N
    real_all = jnp.real(spectrum).reshape(GROUPS, CG, N, N)
    imag_all = jnp.imag(spectrum).reshape(GROUPS, CG, N, N)

    def one_group(pieces):
        return degrid(pieces[0], pieces[1], pieces[2], pieces[3])
    forward = lax.map(one_group, (real_all, imag_all, kernel_weights, tile_index)).reshape(L, 2, NVIS)
    data_next = data_step(data_dual, forward, visibilities, radius_scale)
    return (wavelet_next, lowrank_next, data_next)
```

```python
import math

import jax
import jax.numpy as jnp
import ml_dtypes
import numpy as np
from jax import lax
from jax.experimental import pallas as pl
from jax.experimental.pallas import tpu as pltpu
from jax.sharding import PartitionSpec as P

NSTEP = 5
KT = 16
MIB = 1 << 20

low_taps = (
    -0.010597401784997278,
    0.032883011666982945,
    0.030841381835986965,
    -0.18703481171888114,
    -0.02798376941698385,
    0.6308807679295904,
    0.7148465705525415,
    0.23037781330885523,
)
high_taps = tuple(((-1.0) ** offset * low_taps[7 - offset] for offset in range(8)))
f32 = jnp.float32
bf16 = jnp.bfloat16


def params(mib):
    return pltpu.CompilerParams(vmem_limit_bytes=mib * MIB)


def cost(flops, nbytes):
    return pl.CostEstimate(flops=int(flops), bytes_accessed=int(nbytes), transcendentals=0)


def halves(values):
    upper = values.astype(bf16)
    return upper, (values - upper.astype(f32)).astype(bf16)


def host_halves(values):
    values = values.astype(np.float32)
    upper = values.astype(ml_dtypes.bfloat16)
    return upper, (values - upper.astype(np.float32)).astype(ml_dtypes.bfloat16)


def mm(a, b):
    return jnp.dot(a, b, preferred_element_type=f32)


def mm_t(a, b):
    return lax.dot_general(a, b, (((1,), (1,)), ((), ())), preferred_element_type=f32)


def mm3(a, b):
    ah, al = halves(a)
    bh, bl = halves(b)
    return mm(ah, bh) + (mm(ah, bl) + mm(al, bh))


def swap_chunks(parts, width):
    count = len(parts)
    lane = lax.broadcasted_iota(jnp.int32, parts[0].shape, len(parts[0].shape) - 1)
    axis = len(parts[0].shape) - 1
    step = count // 2
    while step:
        span = step * width
        first = (lane // span) % 2 == 0
        out = list(parts)
        for a in range(count):
            if a & step:
                continue
            b = a | step
            out[a] = jnp.where(first, parts[a], pltpu.roll(parts[b], span, axis))
            out[b] = jnp.where(first, pltpu.roll(parts[a], 128 - span, axis), parts[b])
        parts = out
        step //= 2
    return parts


def pack_kernel(sky_ref, out_ref):
    for quarter in range(4):
        lanes = slice(128 * quarter, 128 * quarter + 128)
        parts = [sky_ref[:, 8 * k : 8 * k + 8, lanes] for k in range(4)]
        for s, done in enumerate(swap_chunks(parts, 32)):
            out_ref[4 * quarter + s] = done


def pack_sky(sky):
    return pl.pallas_call(
        pack_kernel,
        out_shape=jax.ShapeDtypeStruct((16, 16, 8, 128), f32),
        compiler_params=params(16),
        cost_estimate=cost(3e6, 2 * MIB),
        name="pack_sky",
    )(sky)


def gram_kernel(got_ref, dual_ref, y_ref, gram_ref):
    total = jnp.zeros((256, 256), f32)
    for low in range(8):
        seen = got_ref[pl.ds(low, 256, stride=8), :].T
        blocks = []
        for high in range(4):
            rows = pl.ds((8 * high + low) * 32, 32)
            block = dual_ref[rows, :] + 0.5 * seen[32 * high : 32 * high + 32, :]
            y_ref[rows, :] = block
            blocks.append(block)
        right = jnp.concatenate(blocks, axis=0)
        rh, rl = halves(right)
        left = right.T
        lh, ll = halves(left)
        total = total + (mm(lh, rh) + (mm(lh, rl) + mm(ll, rh)))
    gram_ref[...] = total


def gram_part(got, dual):
    return pl.pallas_call(
        gram_kernel,
        out_shape=(
            jax.ShapeDtypeStruct((1024, 256), f32),
            jax.ShapeDtypeStruct((256, 256), f32),
        ),
        compiler_params=params(24),
        cost_estimate=cost(4e8, 3 * MIB),
        name="gram_part",
    )(got, dual)


def mix_kernel(pixels, gram_ref, y_ref, out_ref):
    size = 256
    rows = lax.broadcasted_iota(jnp.int32, (size, size), 0)
    cols = lax.broadcasted_iota(jnp.int32, (size, size), 1)
    identity = (rows == cols).astype(f32)
    shifted = identity + gram_ref[...] * (1.0 / pixels)
    frob = jnp.sqrt(jnp.sum(shifted * shifted, keepdims=True))
    current = shifted / frob
    middle = 1.5 * identity - 0.5 * current
    current = mm3(current, middle)
    inverse = middle
    for turn in range(1, NSTEP):
        middle = 1.5 * identity - 0.5 * mm3(inverse, current)
        if turn < NSTEP - 1:
            current = mm3(current, middle)
        inverse = mm3(middle, inverse)
    mixer = inverse / jnp.sqrt(frob)
    mh, ml = halves(mixer)
    for block in range(4):
        span = pl.ds(256 * block, 256)
        yh, yl = halves(y_ref[span, :])
        out_ref[span, :] = mm_t(yh, mh) + (mm_t(yh, ml) + mm_t(yl, mh))


def mix(gram, y, pixels):
    return pl.pallas_call(
        lambda *refs: mix_kernel(pixels, *refs),
        out_shape=jax.ShapeDtypeStruct((1024, 256), f32),
        compiler_params=params(24),
        cost_estimate=cost(2e9, 3 * MIB),
        name="mix",
    )(gram, y)


def fir(shifted, filter_taps):
    summed = filter_taps[0] * shifted[0]
    for offset in range(1, 8):
        summed = summed + filter_taps[offset] * shifted[offset]
    return summed


def blend_kernel(margin_ref, sky_ref, rim_ref, dual_ref, blend_ref, energy_ref):
    margin = margin_ref[0]
    row = lax.broadcasted_iota(jnp.int32, (8, 512), 0)
    lane = lax.broadcasted_iota(jnp.int32, (32, 512), 1)
    kept = row >= 8 - margin

    @pl.when(pl.program_id(0) == 0)
    def _():
        energy_ref[...] = jnp.zeros_like(energy_ref)

    for c in range(sky_ref.shape[0]):
        ext = jnp.concatenate([jnp.where(kept, rim_ref[c], 0.0), sky_ref[c]], axis=0)
        moved = [ext[8:]] + [pltpu.roll(ext, m, 0)[8:] for m in range(1, 8)]
        for high in range(2):
            value = fir(moved, high_taps if high else low_taps)
            cols = [value] + [
                jnp.where(lane >= m, pltpu.roll(value, m, 1), 0.0) for m in range(1, 8)
            ]
            for band in range(2):
                which = 2 * high + band
                blended = dual_ref[which, c] + 0.5 * fir(cols, high_taps if band else low_taps)
                blend_ref[which, c] = blended
                energy_ref[which] += blended * blended


def blend(margin, sky, rim, dual):
    per = 2
    return pl.pallas_call(
        blend_kernel,
        grid=(16 // per,),
        in_specs=[
            pl.BlockSpec(memory_space=pltpu.SMEM),
            pl.BlockSpec((per, 32, 512), lambda i: (i, 0, 0)),
            pl.BlockSpec((per, 8, 512), lambda i: (i, 0, 0)),
            pl.BlockSpec((4, per, 32, 512), lambda i: (0, i, 0, 0)),
        ],
        out_specs=(
            pl.BlockSpec((4, per, 32, 512), lambda i: (0, i, 0, 0)),
            pl.BlockSpec((4, 32, 512), lambda i: (0, 0, 0)),
        ),
        out_shape=(
            jax.ShapeDtypeStruct((4, 16, 32, 512), f32),
            jax.ShapeDtypeStruct((4, 32, 512), f32),
        ),
        compiler_params=params(16),
        cost_estimate=cost(3e7, 10 * MIB),
        name="blend",
    )(margin, sky, rim, dual)


def shrink_kernel(channels, energy_ref, weight_ref, blend_ref, out_ref):
    ratio = jnp.sqrt(energy_ref[0] * (1.0 / channels)) / weight_ref[0]
    scale = 1.0 / jnp.maximum(1.0, ratio)
    for c in range(blend_ref.shape[1]):
        out_ref[0, c] = blend_ref[0, c] * scale


def shrink(energy, weights, blended, channels):
    return pl.pallas_call(
        lambda *refs: shrink_kernel(channels, *refs),
        grid=(4, 2),
        in_specs=[
            pl.BlockSpec((1, 32, 512), lambda b, i: (b, 0, 0)),
            pl.BlockSpec((1, 32, 512), lambda b, i: (b, 0, 0)),
            pl.BlockSpec((1, 8, 32, 512), lambda b, i: (b, i, 0, 0)),
        ],
        out_specs=pl.BlockSpec((1, 8, 32, 512), lambda b, i: (b, i, 0, 0)),
        out_shape=jax.ShapeDtypeStruct((4, 16, 32, 512), f32),
        input_output_aliases={2: 0},
        compiler_params=params(16),
        cost_estimate=cost(2e6, 9 * MIB),
        name="shrink",
    )(energy, weights, blended)


def degrid_tables(side):
    count = np.arange(side, dtype=np.int64)
    angle = (count[:, None] * count[None, :] % side) * (2.0 * np.pi / side)
    cos_h, cos_l = host_halves(np.cos(angle))
    sin_h, sin_l = host_halves(np.sin(angle))
    ky, row = np.arange(16)[:, None], np.arange(32)[None, :]
    turn = ky * row * (2.0 * np.pi / side)
    whole = np.zeros((16, 4, 2, 2, 4, 32))
    for ch in range(4):
        whole[:, ch, 0, 0, ch, :] = np.cos(turn)
        whole[:, ch, 0, 1, ch, :] = np.sin(turn)
        whole[:, ch, 1, 0, ch, :] = -np.sin(turn)
        whole[:, ch, 1, 1, ch, :] = np.cos(turn)
    row_h, row_l = host_halves(whole.reshape(128, 256))
    return cos_h, cos_l, sin_h, sin_l, row_h, row_l


def degrid_kernel(
    tx_ref,
    turn_ref,
    sky_ref,
    weight_ref,
    pc_ref,
    ps_ref,
    ch_ref,
    cl_ref,
    sh_ref,
    sl_ref,
    rh_ref,
    rl_ref,
    out_ref,
    xh_ref,
    xl_ref,
    table_ref,
    pre_ref,
    pim_ref,
    t_ref,
    u_ref,
):
    for b in range(32):
        start = pl.multiple_of(tx_ref[b] * KT, KT)
        for k, ref in enumerate((ch_ref, cl_ref, sh_ref, sl_ref)):
            table_ref[k, KT * b : KT * b + KT, :] = ref[pl.ds(start, KT), :]
    xh, xl = halves(sky_ref[...].reshape(512, 512))
    xh_ref[...] = xh
    xl_ref[...] = xl
    for half in range(4):
        rows = slice(128 * half, 128 * half + 128)
        xh, xl = xh_ref[rows, :], xl_ref[rows, :]
        gc = mm_t(xh, table_ref[0]) + (mm_t(xl, table_ref[0]) + mm_t(xh, table_ref[1]))
        gs = mm_t(xh, table_ref[2]) + (mm_t(xl, table_ref[2]) + mm_t(xh, table_ref[3]))
        gc, gs = gc.reshape(4, 32, 512), gs.reshape(4, 32, 512)
        pc, ps = pc_ref[...][None], ps_ref[...][None]
        pre = (gc * pc - gs * ps).reshape(128, 512)
        pim = (-(gs * pc + gc * ps)).reshape(128, 512)
        both_h, both_l = halves(jnp.concatenate([pre, pim], axis=0))
        t_ref[half] = mm(rh_ref[...], both_h) + (mm(rl_ref[...], both_h) + mm(rh_ref[...], both_l))
    even = lax.broadcasted_iota(jnp.int32, (8, 128), 0) % 2 == 0
    for quarter in range(4):
        for four in range(4):
            for high in range(2):
                parts = []
                for low in range(8):
                    ky = 8 * high + low
                    part = t_ref[four, 8 * ky : 8 * ky + 8, 128 * quarter : 128 * quarter + 128]
                    other = jnp.where(even, pltpu.roll(part, 7, 0), -pltpu.roll(part, 1, 0))
                    parts.append(part * turn_ref[0, ky] + other * turn_ref[1, ky])
                for b, done in enumerate(swap_chunks(parts, 16)):
                    u_ref[32 * b + 8 * four : 32 * b + 8 * four + 8, 128 * high : 128 * high + 128] = done
        uh, ul = halves(u_ref[...])
        rows = slice(256 * quarter, 256 * quarter + 256)
        sums = []
        for part in range(2):
            weights = weight_ref[rows, 256 * part : 256 * part + 256]
            sums.append(mm_t(uh, weights) + mm_t(ul, weights))
        lane = lax.broadcasted_iota(jnp.int32, (32, 256), 1)
        row = lax.broadcasted_iota(jnp.int32, (32, 256), 0)
        first = jnp.zeros((32, 256), f32)
        second = jnp.zeros((32, 256), f32)
        for b in range(8):
            mine = lane // 32 == b
            first = jnp.where(mine, sums[0][32 * b : 32 * b + 32, :], first)
            second = jnp.where(mine, sums[1][32 * b : 32 * b + 32, :], second)
        other = jnp.where(row % 2 == 0, -pltpu.roll(second, 31, 0), pltpu.roll(second, 1, 0))
        out_ref[:, 256 * quarter : 256 * quarter + 256] = (first + other) * (1.0 / 512.0)


def degrid(sky, weights, tile_ids, facet):
    side = sky.shape[-1]
    tables = [jnp.asarray(t) for t in degrid_tables(side)]
    tx = tile_ids % 32
    ty = tile_ids // 32
    ty_lanes = jnp.repeat(ty, KT)
    row = jnp.arange(32, dtype=jnp.int32)
    angle = (ty_lanes[None, :] * row[:, None] % 32).astype(f32) * (2.0 * math.pi / 32)
    ky = jnp.arange(KT, dtype=jnp.int32)
    facet_angle = (ky * facet % 16).astype(f32) * (2.0 * math.pi / 16)
    turn = jnp.stack([jnp.cos(facet_angle), jnp.sin(facet_angle)])
    smem = pl.BlockSpec(memory_space=pltpu.SMEM)
    vmem = pl.BlockSpec(memory_space=pltpu.VMEM)
    return pl.pallas_call(
        degrid_kernel,
        in_specs=[smem, smem] + [vmem] * 10,
        out_specs=vmem,
        out_shape=jax.ShapeDtypeStruct((32, 1024), f32),
        scratch_shapes=[
            pltpu.VMEM((512, 512), bf16),
            pltpu.VMEM((512, 512), bf16),
            pltpu.VMEM((4, 512, 512), bf16),
            pltpu.VMEM((8, 128), f32),
            pltpu.VMEM((8, 128), f32),
            pltpu.VMEM((4, 128, 512), f32),
            pltpu.VMEM((256, 256), f32),
        ],
        compiler_params=params(40),
        cost_estimate=cost(3e9, 6 * MIB),
        name="degrid",
    )(tx, turn, sky, weights, jnp.cos(angle), jnp.sin(angle), *tables)


def data_step(data_dual, forward, visibilities, radius_scale):
    moved = data_dual + forward
    residual = 2.0 * moved - visibilities
    distance = jnp.sqrt(jnp.sum(residual * residual, axis=(1, 2)) + 1e-06)
    radius = radius_scale * math.sqrt(2.0 * visibilities.shape[2])
    shrunk = jnp.minimum(1.0, radius / distance)
    return moved - 0.5 * (visibilities + residual * shrunk[:, None, None])


def trade(values, axis):
    return lax.all_to_all(values, axis, 0, 0, tiled=True)


def spread(values, axis):
    count = lax.axis_size(axis)
    return trade(jnp.broadcast_to(values[None], (count,) + values.shape), axis)


def per_device(
    sky_image,
    margins,
    wavelet_dual,
    sparsity_weights,
    lowrank_dual,
    kernel_weights,
    tile_index,
    data_dual,
    visibilities,
    radius_scale,
):
    facet_rows, image_side = sky_image.shape[1:]
    channels = lowrank_dual.shape[0]
    facet = lax.axis_index("facet")
    devices = lax.axis_size("facet")

    got = trade(pack_sky(sky_image), "chan").reshape(2048, 128)
    rim = lax.ppermute(
        sky_image[:, facet_rows - 8 :, :], "facet", [(i, i + 1) for i in range(devices - 1)]
    )
    margin = lax.dynamic_slice(margins, (facet,), (1,))
    blended, energy_part = blend(margin, sky_image, rim, wavelet_dual)

    forward_part = degrid(sky_image, kernel_weights.reshape(1024, 512), tile_index[0], facet)
    forward = jnp.sum(trade(forward_part.reshape(16, 2, 1024), "facet"), axis=0, keepdims=True)
    data_next = data_step(data_dual, forward, visibilities, radius_scale)

    energy_own = jnp.sum(trade(energy_part.reshape(16, 8, 512), "chan"), axis=0)
    energy = spread(energy_own, "chan").reshape(4, 32, 512)
    wavelet_next = shrink(energy, sparsity_weights, blended, channels)

    dual = jnp.transpose(lowrank_dual, (1, 2, 0)).reshape(1024, 256)
    y, part = gram_part(got, dual)
    gram_own = jnp.sum(trade(part.reshape(16, 16, 256), "chan"), axis=0)
    gram = spread(gram_own, "chan").reshape(256, 256)
    mixed = mix(gram, y, facet_rows * image_side)
    lowrank_next = jnp.transpose(mixed.reshape(32, 32, 256), (2, 0, 1))
    return (wavelet_next, lowrank_next, data_next)


def solution(mesh):
    in_specs = (
        P("chan", "facet", None),
        P(),
        P(None, "chan", "facet", None),
        P(None, "facet", None),
        P(None, "facet", "chan"),
        P("chan", None, None, None),
        P("chan", None),
        P(("chan", "facet"), None, None),
        P(("chan", "facet"), None, None),
        P(("chan", "facet")),
    )
    out_specs = (
        P(None, "chan", "facet", None),
        P(None, "facet", "chan"),
        P(("chan", "facet"), None, None),
    )
    return jax.shard_map(
        per_device, mesh=mesh, in_specs=in_specs, out_specs=out_specs, check_vma=False
    )
```

```python
import math

import jax
import jax.numpy as jnp
import ml_dtypes
import numpy as np
from jax import lax
from jax.experimental import pallas as pl
from jax.experimental.pallas import tpu as pltpu
from jax.sharding import PartitionSpec as P

NSTEP = 5
KT = 16
MIB = 1 << 20
BIG = 56

low_taps = (
    -0.010597401784997278,
    0.032883011666982945,
    0.030841381835986965,
    -0.18703481171888114,
    -0.02798376941698385,
    0.6308807679295904,
    0.7148465705525415,
    0.23037781330885523,
)
high_taps = tuple(((-1.0) ** offset * low_taps[7 - offset] for offset in range(8)))
f32 = jnp.float32
bf16 = jnp.bfloat16


def params(mib):
    return pltpu.CompilerParams(vmem_limit_bytes=int(mib * MIB))


def cost(flops, nbytes):
    return pl.CostEstimate(flops=int(flops), bytes_accessed=int(nbytes), transcendentals=0)


def halves(values):
    upper = values.astype(bf16)
    return upper, (values - upper.astype(f32)).astype(bf16)


def host_halves(values):
    values = values.astype(np.float32)
    upper = values.astype(ml_dtypes.bfloat16)
    return upper, (values - upper.astype(np.float32)).astype(ml_dtypes.bfloat16)


def mm(a, b):
    return jnp.dot(a, b, preferred_element_type=f32)


def mm_t(a, b):
    return lax.dot_general(a, b, (((1,), (1,)), ((), ())), preferred_element_type=f32)


def mm3(a, b):
    ah, al = halves(a)
    bh, bl = halves(b)
    return mm(ah, bh) + (mm(ah, bl) + mm(al, bh))


def swap_chunks(parts, width):
    count = len(parts)
    lane = lax.broadcasted_iota(jnp.int32, parts[0].shape, len(parts[0].shape) - 1)
    axis = len(parts[0].shape) - 1
    step = count // 2
    while step:
        span = step * width
        first = (lane // span) % 2 == 0
        out = list(parts)
        for a in range(count):
            if a & step:
                continue
            b = a | step
            out[a] = jnp.where(first, parts[a], pltpu.roll(parts[b], span, axis))
            out[b] = jnp.where(first, pltpu.roll(parts[a], 128 - span, axis), parts[b])
        parts = out
        step //= 2
    return parts


def pack_kernel(sky_in, packed_out, sky_ref, packed_ref, in_sems, out_sems):
    fours = [slice(4 * k, 4 * k + 4) for k in range(4)]
    coming = [
        pltpu.make_async_copy(sky_in.at[four], sky_ref.at[four], in_sems.at[k])
        for k, four in enumerate(fours)
    ]
    going = [
        pltpu.make_async_copy(packed_ref.at[:, four], packed_out.at[:, four], out_sems.at[k])
        for k, four in enumerate(fours)
    ]
    for copy in coming:
        copy.start()
    for k, four in enumerate(fours):
        coming[k].wait()
        for quarter in range(4):
            lanes = slice(128 * quarter, 128 * quarter + 128)
            parts = [sky_ref[four, 8 * j : 8 * j + 8, lanes] for j in range(4)]
            for s, done in enumerate(swap_chunks(parts, 32)):
                packed_ref[4 * quarter + s, four] = done
        going[k].start()
    for copy in going:
        copy.wait()


def pack_sky(sky):
    hbm = pl.BlockSpec(memory_space=pl.ANY)
    return pl.pallas_call(
        pack_kernel,
        in_specs=[hbm],
        out_specs=hbm,
        out_shape=jax.ShapeDtypeStruct((16, 16, 8, 128), f32),
        scratch_shapes=[
            pltpu.VMEM((16, 32, 512), f32),
            pltpu.VMEM((16, 16, 8, 128), f32),
            pltpu.SemaphoreType.DMA((4,)),
            pltpu.SemaphoreType.DMA((4,)),
        ],
        compiler_params=params(59.9),
        cost_estimate=cost(3e6, 2 * MIB),
        name="pack_sky",
    )(sky)


def gram_kernel(got_ref, dual_ref, energy_ref, y_out, part_out, y_ref, gram_ref, sems):
    copies = [pltpu.make_async_copy(energy_ref, part_out.at[:, :32], sems.at[8])]
    copies[0].start()
    total = jnp.zeros((256, 256), f32)
    for low in range(8):
        seen = got_ref[pl.ds(low, 256, stride=8), :].T
        right = dual_ref[:, low].reshape(128, 256) + 0.5 * seen
        y_ref[:, low] = right.reshape(4, 32, 256)
        copies.append(pltpu.make_async_copy(y_ref.at[:, low], y_out.at[:, low], sems.at[low]))
        copies[-1].start()
        rh, rl = halves(right)
        left = right.T
        lh, ll = halves(left)
        total = total + (mm(lh, rh) + (mm(lh, rl) + mm(ll, rh)))
    for peer in range(16):
        for h in range(2):
            gram_ref[peer, 16 * h : 16 * h + 16, :] = total[
                16 * peer : 16 * peer + 16, 128 * h : 128 * h + 128
            ]
    copies.append(pltpu.make_async_copy(gram_ref, part_out.at[:, 32:], sems.at[9]))
    copies[-1].start()
    for copy in copies:
        copy.wait()


def gram_part(got, dual, energy):
    vmem = pl.BlockSpec(memory_space=pltpu.VMEM)
    hbm = pl.BlockSpec(memory_space=pl.ANY)
    return pl.pallas_call(
        gram_kernel,
        in_specs=[vmem] * 3,
        out_specs=(hbm, hbm),
        out_shape=(
            jax.ShapeDtypeStruct((4, 8, 32, 256), f32),
            jax.ShapeDtypeStruct((16, 64, 128), f32),
        ),
        scratch_shapes=[
            pltpu.VMEM((4, 8, 32, 256), f32),
            pltpu.VMEM((16, 32, 128), f32),
            pltpu.SemaphoreType.DMA((10,)),
        ],
        compiler_params=params(58),
        cost_estimate=cost(4e8, 3 * MIB),
        name="gram_part",
    )(got, dual, energy)


def sum_kernel(got_ref, out_ref):
    total = got_ref[0]
    for peer in range(1, 16):
        total = total + got_ref[peer]
    for peer in range(16):
        out_ref[peer] = total


def sum_copies(got):
    return pl.pallas_call(
        sum_kernel,
        out_shape=jax.ShapeDtypeStruct(got.shape, f32),
        compiler_params=params(16),
        cost_estimate=cost(1e6, MIB),
        name="sum_copies",
    )(got)


def finish_kernel(
    pixels,
    channels,
    got_ref,
    weight_in,
    blend_in,
    y_in,
    wave_out,
    mixed_out,
    weight_ref,
    blend_ref,
    wave_ref,
    y_ref,
    mixed_ref,
    in_sems,
    out_sems,
):
    coming = [pltpu.make_async_copy(weight_in, weight_ref, in_sems.at[5])]
    coming += [
        pltpu.make_async_copy(blend_in.at[band], blend_ref.at[band], in_sems.at[band])
        for band in range(4)
    ]
    coming.append(pltpu.make_async_copy(y_in, y_ref, in_sems.at[4]))
    for copy in coming:
        copy.start()
    going = []

    def wave():
        for copy in coming:
            copy.wait()
        for band in range(4):
            for part in range(4):
                rows = slice(8 * part, 8 * part + 8)
                for q in range(4):
                    lanes = slice(128 * q, 128 * q + 128)
                    energy = got_ref[4 * band + part, 8 * q : 8 * q + 8, :]
                    ratio = jnp.sqrt(energy * (1.0 / channels)) / weight_ref[band, rows, lanes]
                    scale = 1.0 / jnp.maximum(1.0, ratio)
                    wave_ref[band, :, rows, lanes] = blend_ref[band, :, rows, lanes] * scale[None]
            copy = pltpu.make_async_copy(wave_ref.at[band], wave_out.at[band], out_sems.at[band])
            copy.start()
            going.append(copy)

    size = 256
    rows = lax.broadcasted_iota(jnp.int32, (size, size), 0)
    cols = lax.broadcasted_iota(jnp.int32, (size, size), 1)
    identity = (rows == cols).astype(f32)
    sides = [got_ref[:, 32 + 16 * h : 48 + 16 * h, :].reshape(size, 128) for h in range(2)]
    shifted = identity + jnp.concatenate(sides, axis=1) * (1.0 / pixels)
    frob = jnp.sqrt(jnp.sum(shifted * shifted, keepdims=True))
    current = shifted / frob
    middle = 1.5 * identity - 0.5 * current
    current = mm3(current, middle)
    inverse = middle
    for turn in range(1, NSTEP):
        middle = 1.5 * identity - 0.5 * mm3(inverse, current)
        if turn < NSTEP - 1:
            both = mm3(jnp.concatenate([current, inverse], axis=0), middle)
            current, inverse = both[:size], both[size:]
        else:
            inverse = mm3(inverse, middle)
        if turn == 2:
            wave()
    mixer = inverse / jnp.sqrt(frob)
    mh, ml = halves(mixer)
    for block in range(4):
        span = pl.ds(256 * block, 256)
        yh, yl = halves(y_ref[span, :])
        mixed_ref[span, :] = mm_t(yh, mh) + (mm_t(yh, ml) + mm_t(yl, mh))
        copy = pltpu.make_async_copy(mixed_ref.at[span], mixed_out.at[span], out_sems.at[4 + block])
        copy.start()
        going.append(copy)
    for copy in going:
        copy.wait()


def finish(got, weights, blended, y, pixels, channels):
    hbm = pl.BlockSpec(memory_space=pl.ANY)
    return pl.pallas_call(
        lambda *refs: finish_kernel(pixels, channels, *refs),
        in_specs=[pl.BlockSpec(memory_space=pltpu.VMEM), hbm, hbm, hbm],
        out_specs=(hbm, hbm),
        out_shape=(
            jax.ShapeDtypeStruct(blended.shape, f32),
            jax.ShapeDtypeStruct((1024, 256), f32),
        ),
        scratch_shapes=[
            pltpu.VMEM(weights.shape, f32),
            pltpu.VMEM(blended.shape, f32),
            pltpu.VMEM(blended.shape, f32),
            pltpu.VMEM((1024, 256), f32),
            pltpu.VMEM((1024, 256), f32),
            pltpu.SemaphoreType.DMA((6,)),
            pltpu.SemaphoreType.DMA((8,)),
        ],
        compiler_params=params(59.8),
        cost_estimate=cost(2e9, 8 * MIB),
        name="finish",
    )(got, weights, blended, y)


def filter_tables():
    both = (low_taps, high_taps)
    down = np.zeros((2, 4, 32, 4, 40))
    across = np.zeros((256, 2, 128))
    for which, taps in enumerate(both):
        for m, tap in enumerate(taps):
            for row in range(32):
                for ch in range(4):
                    down[which, ch, row, ch, 8 + row - m] = tap
            for col in range(128):
                across[128 + col - m, which, col] = 0.5 * tap
    down = np.concatenate(host_halves(down.reshape(256, 160)))
    return down, np.concatenate(host_halves(across.reshape(256, 256)))


def blend_kernel(margin_ref, sky_ref, rim_ref, dual_ref, down_ref, across_ref, blend_ref, energy_ref):
    row = lax.broadcasted_iota(jnp.int32, (8, 512), 0)
    kept = row >= 8 - margin_ref[0]

    @pl.when(pl.program_id(0) == 0)
    def _():
        energy_ref[...] = jnp.zeros_like(energy_ref)

    pieces = []
    for c in range(4):
        pieces += [jnp.where(kept, rim_ref[c], 0.0), sky_ref[c]]
    eh, el = halves(jnp.concatenate(pieces, axis=0))
    dh, dl = down_ref[:256, :], down_ref[256:, :]
    filtered = mm(dh, eh) + (mm(dh, el) + mm(dl, eh))
    vh, vl = halves(filtered)
    for j in range(4):
        if j:
            lanes = slice(128 * j - 128, 128 * j + 128)
            ah, al = across_ref[:256, :], across_ref[256:, :]
        else:
            lanes = slice(0, 128)
            ah, al = across_ref[128:256, :], across_ref[384:, :]
        done = mm(vh[:, lanes], ah) + (mm(vl[:, lanes], ah) + mm(vh[:, lanes], al))
        here = slice(128 * j, 128 * j + 128)
        for band in range(4):
            part = done[128 * (band // 2) : 128 * (band // 2) + 128]
            part = part[:, 128 * (band % 2) : 128 * (band % 2) + 128].reshape(4, 32, 128)
            blended = dual_ref[band, :, :, here] + part
            blend_ref[band, :, :, here] = blended
            squares = jnp.sum(blended * blended, axis=0)
            for strip in range(4):
                energy_ref[4 * band + strip, 8 * j : 8 * j + 8, :] += squares[8 * strip : 8 * strip + 8]


def blend(margin, sky, rim, dual):
    down, across = (jnp.asarray(t) for t in filter_tables())
    return pl.pallas_call(
        blend_kernel,
        grid=(4,),
        in_specs=[
            pl.BlockSpec(memory_space=pltpu.SMEM),
            pl.BlockSpec((4, 32, 512), lambda i: (i, 0, 0)),
            pl.BlockSpec((4, 8, 512), lambda i: (i, 0, 0)),
            pl.BlockSpec((4, 4, 32, 512), lambda i: (0, i, 0, 0)),
            pl.BlockSpec((512, 160), lambda i: (0, 0)),
            pl.BlockSpec((512, 256), lambda i: (0, 0)),
        ],
        out_specs=(
            pl.BlockSpec((4, 4, 32, 512), lambda i: (0, i, 0, 0)),
            pl.BlockSpec((16, 32, 128), lambda i: (0, 0, 0)),
        ),
        out_shape=(
            jax.ShapeDtypeStruct((4, 16, 32, 512), f32),
            jax.ShapeDtypeStruct((16, 32, 128), f32),
        ),
        compiler_params=params(57),
        cost_estimate=cost(3e9, 10 * MIB),
        name="blend",
    )(margin, sky, rim, dual, down, across)


def degrid_tables(side):
    column = np.arange(side, dtype=np.int64)[None, :]
    kx = np.arange(KT, dtype=np.int64)[:, None]
    tile = np.arange(side // KT, dtype=np.int64)[:, None]
    inner = (kx * column % side) * (2.0 * np.pi / side)
    outer = (KT * tile * column % side) * (2.0 * np.pi / side)
    columns = np.concatenate([np.cos(inner), np.sin(inner), np.cos(outer), np.sin(outer)])
    ky, row = np.arange(16)[:, None], np.arange(32)[None, :]
    turn = ky * row * (2.0 * np.pi / side)
    whole = np.zeros((16, 4, 2, 2, 4, 32))
    for ch in range(4):
        whole[:, ch, 0, 0, ch, :] = np.cos(turn)
        whole[:, ch, 0, 1, ch, :] = np.sin(turn)
        whole[:, ch, 1, 0, ch, :] = -np.sin(turn)
        whole[:, ch, 1, 1, ch, :] = np.cos(turn)
    rows = np.concatenate(host_halves(whole.reshape(128, 256)))
    return columns.astype(np.float32), rows


def channel_at(place):
    b0, b3, b1, b2 = ((place >> k) & 1 for k in (3, 2, 1, 0))
    return b0 + 2 * b1 + 4 * b2 + 8 * b3


def degrid_kernel(
    tx_ref,
    turn_ref,
    sky_ref,
    phase_ref,
    column_ref,
    row_ref,
    weight_in,
    out_ref,
    xh_ref,
    xl_ref,
    table_ref,
    t_ref,
    u_ref,
    weight_ref,
    sem,
):
    coming = pltpu.make_async_copy(weight_in, weight_ref, sem.at[0])
    coming.start()
    inner_cos, inner_sin = column_ref[:KT, :], column_ref[KT : 2 * KT, :]
    for b in range(32):
        outer_cos = column_ref[pl.ds(2 * KT + tx_ref[b], 1), :]
        outer_sin = column_ref[pl.ds(2 * KT + 32 + tx_ref[b], 1), :]
        rows = slice(KT * b, KT * b + KT)
        both = (
            inner_cos * outer_cos - inner_sin * outer_sin,
            inner_sin * outer_cos + inner_cos * outer_sin,
        )
        for k, values in enumerate(both):
            upper, lower = halves(values)
            table_ref[2 * k, rows, :] = upper
            table_ref[2 * k + 1, rows, :] = lower
    for place in range(16):
        xh, xl = halves(sky_ref[channel_at(place)])
        xh_ref[32 * place : 32 * place + 32, :] = xh
        xl_ref[32 * place : 32 * place + 32, :] = xl
    cos_h, cos_l, sin_h, sin_l = (table_ref[k] for k in range(4))
    row_h, row_l = row_ref[:128, :], row_ref[128:, :]
    for half in range(4):
        rows = slice(128 * half, 128 * half + 128)
        xh, xl = xh_ref[rows, :], xl_ref[rows, :]
        gc = mm_t(xh, cos_h) + (mm_t(xl, cos_h) + mm_t(xh, cos_l))
        gs = mm_t(xh, sin_h) + (mm_t(xl, sin_h) + mm_t(xh, sin_l))
        gc, gs = gc.reshape(4, 32, 512), gs.reshape(4, 32, 512)
        pc, ps = phase_ref[0][None], phase_ref[1][None]
        pre = (gc * pc - gs * ps).reshape(128, 512)
        pim = (-(gs * pc + gc * ps)).reshape(128, 512)
        both_h, both_l = halves(jnp.concatenate([pre, pim], axis=0))
        t_ref[half] = mm(row_h, both_h) + (mm(row_l, both_h) + mm(row_h, both_l))
    even = lax.broadcasted_iota(jnp.int32, (8, 128), 0) % 2 == 0
    coming.wait()
    for quarter in range(4):
        for four in range(4):
            for high in range(2):
                parts = []
                for low in range(8):
                    ky = 8 * high + low
                    part = t_ref[four, 8 * ky : 8 * ky + 8, 128 * quarter : 128 * quarter + 128]
                    other = jnp.where(even, pltpu.roll(part, 7, 0), -pltpu.roll(part, 1, 0))
                    parts.append(part * turn_ref[0, ky] + other * turn_ref[1, ky])
                for b, done in enumerate(swap_chunks(parts, 16)):
                    u_ref[32 * b + 8 * four : 32 * b + 8 * four + 8, 128 * high : 128 * high + 128] = done
        uh, ul = halves(u_ref[...])
        rows = slice(256 * quarter, 256 * quarter + 256)
        sums = []
        for part in range(2):
            weights = weight_ref[rows, 256 * part : 256 * part + 256]
            sums.append(mm_t(uh, weights) + mm_t(ul, weights))
        lane = lax.broadcasted_iota(jnp.int32, (32, 256), 1)
        row = lax.broadcasted_iota(jnp.int32, (32, 256), 0)
        first = jnp.zeros((32, 256), f32)
        second = jnp.zeros((32, 256), f32)
        for b in range(8):
            mine = lane // 32 == b
            first = jnp.where(mine, sums[0][32 * b : 32 * b + 32, :], first)
            second = jnp.where(mine, sums[1][32 * b : 32 * b + 32, :], second)
        other = jnp.where(row % 2 == 0, -pltpu.roll(second, 31, 0), pltpu.roll(second, 1, 0))
        out_ref[:, 256 * quarter : 256 * quarter + 256] = (first + other) * (1.0 / 512.0)


def degrid(sky, weights, tile_ids, facet):
    side = sky.shape[-1]
    columns, rows = (jnp.asarray(t) for t in degrid_tables(side))
    ty_lanes = jnp.repeat(tile_ids // 32, KT)
    row = jnp.arange(32, dtype=jnp.int32)
    angle = (ty_lanes[None, :] * row[:, None] % 32).astype(f32) * (2.0 * math.pi / 32)
    phase = jnp.stack([jnp.cos(angle), jnp.sin(angle)])
    ky = jnp.arange(KT, dtype=jnp.int32)
    facet_angle = (ky * facet % 16).astype(f32) * (2.0 * math.pi / 16)
    turn = jnp.stack([jnp.cos(facet_angle), jnp.sin(facet_angle)])
    smem = pl.BlockSpec(memory_space=pltpu.SMEM)
    vmem = pl.BlockSpec(memory_space=pltpu.VMEM)
    return pl.pallas_call(
        degrid_kernel,
        in_specs=[smem, smem] + [vmem] * 4 + [pl.BlockSpec(memory_space=pl.ANY)],
        out_specs=vmem,
        out_shape=jax.ShapeDtypeStruct((32, 1024), f32),
        scratch_shapes=[
            pltpu.VMEM((512, 512), bf16),
            pltpu.VMEM((512, 512), bf16),
            pltpu.VMEM((4, 512, 512), bf16),
            pltpu.VMEM((4, 128, 512), f32),
            pltpu.VMEM((256, 256), f32),
            pltpu.VMEM((1024, 512), bf16),
            pltpu.SemaphoreType.DMA((1,)),
        ],
        compiler_params=params(24),
        cost_estimate=cost(3e9, 6 * MIB),
        name="degrid",
    )(tile_ids % 32, turn, sky, phase, columns, rows, weights)


def data_step(data_dual, forward, visibilities, radius_scale):
    moved = data_dual + forward
    residual = 2.0 * moved - visibilities
    distance = jnp.sqrt(jnp.sum(residual * residual, axis=(1, 2)) + 1e-06)
    radius = radius_scale * math.sqrt(2.0 * visibilities.shape[2])
    shrunk = jnp.minimum(1.0, radius / distance)
    return moved - 0.5 * (visibilities + residual * shrunk[:, None, None])


def trade(values, axis):
    return lax.all_to_all(values, axis, 0, 0, tiled=True)


def halving_sum(values, axis, bits):
    me = lax.axis_index(axis)
    count = lax.axis_size(axis)
    for bit in bits:
        values = values.reshape((2, values.shape[0] // 2) + values.shape[1:])
        mine = (me >> bit) & 1
        sent = lax.dynamic_index_in_dim(values, 1 - mine, 0, keepdims=False)
        kept = lax.dynamic_index_in_dim(values, mine, 0, keepdims=False)
        pairs = [(i, i ^ (1 << bit)) for i in range(count)]
        values = kept + lax.ppermute(sent, axis, pairs)
    return values[0]


def per_device(
    sky_image,
    margins,
    wavelet_dual,
    sparsity_weights,
    lowrank_dual,
    kernel_weights,
    tile_index,
    data_dual,
    visibilities,
    radius_scale,
):
    facet_rows, image_side = sky_image.shape[1:]
    channels = lowrank_dual.shape[0]
    facet = lax.axis_index("facet")
    devices = lax.axis_size("facet")

    packed, sky = lax.optimization_barrier((pack_sky(sky_image), sky_image))
    got = trade(packed, "chan").reshape(2048, 128)
    rim = lax.ppermute(
        sky[:, facet_rows - 8 :, :], "facet", [(i, i + 1) for i in range(devices - 1)]
    )
    forward_part = degrid(sky, kernel_weights.reshape(1024, 512), tile_index[0], facet)
    margin = lax.dynamic_slice(margins, (facet,), (1,))
    margin, forward_part = lax.optimization_barrier((margin, forward_part))
    blended, energy_part = blend(margin, sky, rim, wavelet_dual)
    energy_part, forward_part = lax.optimization_barrier((energy_part, forward_part))
    forward = halving_sum(forward_part.reshape(16, 2, 1024), "facet", (0, 3, 1, 2))[None]

    dual = jnp.transpose(lowrank_dual, (1, 2, 0)).reshape(4, 8, 32, 256)
    y, part = gram_part(got, dual, energy_part)
    reduced, forward = lax.optimization_barrier((trade(part, "chan"), forward))
    data_next = data_step(data_dual, forward, visibilities, radius_scale)
    total = trade(sum_copies(reduced), "chan")
    wavelet_next, mixed = finish(
        total, sparsity_weights, blended, y.reshape(1024, 256), facet_rows * image_side, channels
    )
    lowrank_next = jnp.transpose(mixed.reshape(32, 32, 256), (2, 0, 1))
    return (wavelet_next, lowrank_next, data_next)


def solution(mesh):
    in_specs = (
        P("chan", "facet", None),
        P(),
        P(None, "chan", "facet", None),
        P(None, "facet", None),
        P(None, "facet", "chan"),
        P("chan", None, None, None),
        P("chan", None),
        P(("chan", "facet"), None, None),
        P(("chan", "facet"), None, None),
        P(("chan", "facet")),
    )
    out_specs = (
        P(None, "chan", "facet", None),
        P(None, "facet", "chan"),
        P(("chan", "facet"), None, None),
    )
    return jax.shard_map(
        per_device, mesh=mesh, in_specs=in_specs, out_specs=out_specs, check_vma=False
    )
```

```python
import math

import jax
import jax.numpy as jnp
import ml_dtypes
import numpy as np
from jax import lax
from jax.experimental import pallas as pl
from jax.experimental.pallas import tpu as pltpu
from jax.sharding import PartitionSpec as P

NSTEP = 5
KT = 16
MIB = 1 << 20
ROOM = 24

low_taps = (
    -0.010597401784997278,
    0.032883011666982945,
    0.030841381835986965,
    -0.18703481171888114,
    -0.02798376941698385,
    0.6308807679295904,
    0.7148465705525415,
    0.23037781330885523,
)
high_taps = tuple(((-1.0) ** offset * low_taps[7 - offset] for offset in range(8)))
f32 = jnp.float32
bf16 = jnp.bfloat16


def params(mib):
    return pltpu.CompilerParams(vmem_limit_bytes=int(mib * MIB))


def cost(flops, nbytes):
    return pl.CostEstimate(flops=int(flops), bytes_accessed=int(nbytes), transcendentals=0)


def halves(values):
    upper = values.astype(bf16)
    return upper, (values - upper.astype(f32)).astype(bf16)


def host_halves(values):
    values = values.astype(np.float32)
    upper = values.astype(ml_dtypes.bfloat16)
    return upper, (values - upper.astype(np.float32)).astype(ml_dtypes.bfloat16)


def mm(a, b):
    return jnp.dot(a, b, preferred_element_type=f32)


def mm_t(a, b):
    return lax.dot_general(a, b, (((1,), (1,)), ((), ())), preferred_element_type=f32)


def mm3_right(a, bh, bl):
    ah, al = halves(a)
    return mm(ah, bh) + (mm(ah, bl) + mm(al, bh))


def swap_chunks(parts, width):
    count = len(parts)
    lane = lax.broadcasted_iota(jnp.int32, parts[0].shape, len(parts[0].shape) - 1)
    axis = len(parts[0].shape) - 1
    step = count // 2
    while step:
        span = step * width
        first = (lane // span) % 2 == 0
        out = list(parts)
        for a in range(count):
            if a & step:
                continue
            b = a | step
            out[a] = jnp.where(first, parts[a], pltpu.roll(parts[b], span, axis))
            out[b] = jnp.where(first, pltpu.roll(parts[a], 128 - span, axis), parts[b])
        parts = out
        step //= 2
    return parts


def pack_kernel(sky_in, packed_out, rim_out, sky_ref, packed_ref, in_sems, out_sems):
    fours = [slice(4 * k, 4 * k + 4) for k in range(4)]
    coming = [
        pltpu.make_async_copy(sky_in.at[four], sky_ref.at[four], in_sems.at[k])
        for k, four in enumerate(fours)
    ]
    going = [
        pltpu.make_async_copy(packed_ref.at[:, four], packed_out.at[:, four], out_sems.at[k])
        for k, four in enumerate(fours)
    ]
    going.append(pltpu.make_async_copy(sky_ref.at[:, 24:, :], rim_out, out_sems.at[4]))
    for copy in coming:
        copy.start()
    for k, four in enumerate(fours):
        coming[k].wait()
        for quarter in range(4):
            lanes = slice(128 * quarter, 128 * quarter + 128)
            parts = [sky_ref[four, 8 * j : 8 * j + 8, lanes] for j in range(4)]
            for s, done in enumerate(swap_chunks(parts, 32)):
                packed_ref[4 * quarter + s, four] = done
        going[k].start()
    going[4].start()
    for copy in going:
        copy.wait()


def pack_sky(sky):
    hbm = pl.BlockSpec(memory_space=pl.ANY)
    return pl.pallas_call(
        pack_kernel,
        in_specs=[hbm],
        out_specs=(hbm, hbm),
        out_shape=(
            jax.ShapeDtypeStruct((16, 16, 8, 128), f32),
            jax.ShapeDtypeStruct((16, 8, 512), f32),
        ),
        scratch_shapes=[
            pltpu.VMEM((16, 32, 512), f32),
            pltpu.VMEM((16, 16, 8, 128), f32),
            pltpu.SemaphoreType.DMA((4,)),
            pltpu.SemaphoreType.DMA((5,)),
        ],
        compiler_params=params(60),
        cost_estimate=cost(3e6, 2 * MIB),
        name="pack_sky",
    )(sky)


def gram_kernel(
    got_ref, dual_ref, kept_ref, other_ref, y_out, part_out, y_ref, sum_ref, gram_ref, sems
):
    sum_ref[...] = kept_ref[...] + other_ref[...]
    copies = [pltpu.make_async_copy(sum_ref, part_out.at[:, :16], sems.at[8])]
    copies[0].start()
    total = jnp.zeros((256, 256), f32)
    cross = jnp.zeros((256, 256), f32)
    held = []
    for low in range(8):
        seen = got_ref[pl.ds(low, 256, stride=8), :].T
        right = dual_ref[:, low].reshape(128, 256) + 0.5 * seen
        rh, rl = halves(right)
        y_ref[0, :, low] = rh.reshape(4, 32, 256)
        y_ref[1, :, low] = rl.reshape(4, 32, 256)
        copies.append(pltpu.make_async_copy(y_ref.at[:, :, low], y_out.at[:2, :, low], sems.at[low]))
        copies[-1].start()
        held.append((rh, rl))
        if low % 4 == 3:
            rh = jnp.concatenate([upper for upper, _ in held], axis=0)
            rl = jnp.concatenate([lower for _, lower in held], axis=0)
            held = []
            lh = rh.T
            total = total + mm(lh, rh)
            cross = cross + mm(lh, rl)
    total = total + (cross + cross.T)
    gram_ref[:, 16:, :] = jnp.zeros((16, 8, 128), f32)
    for peer in range(16):
        turned = total[16 * peer : 16 * peer + 16, :]
        if peer:
            turned = pltpu.roll(turned, 256 - 16 * peer, 1)
        gram_ref[peer, :16, :] = turned[:, :128]
        gram_ref[peer, 16:, :16] = turned[:8, 128:144]
        gram_ref[peer, 16:, 16:32] = turned[8:, 128:144]
    copies.append(pltpu.make_async_copy(gram_ref, part_out.at[:, 16:], sems.at[9]))
    copies[-1].start()
    for copy in copies:
        copy.wait()


def gram_part(got, dual, kept, other):
    vmem = pl.BlockSpec(memory_space=pltpu.VMEM)
    hbm = pl.BlockSpec(memory_space=pl.ANY)
    return pl.pallas_call(
        gram_kernel,
        in_specs=[vmem] * 4,
        out_specs=(hbm, hbm),
        out_shape=(
            jax.ShapeDtypeStruct((2 * ROOM, 4, 8, 32, 256), bf16),
            jax.ShapeDtypeStruct((16, 40, 128), f32),
        ),
        scratch_shapes=[
            pltpu.VMEM((2, 4, 8, 32, 256), bf16),
            pltpu.VMEM((16, 16, 128), f32),
            pltpu.VMEM((16, 24, 128), f32),
            pltpu.SemaphoreType.DMA((10,)),
        ],
        compiler_params=params(40),
        cost_estimate=cost(4e8, 3 * MIB),
        name="gram_part",
    )(got, dual, kept, other)


def sum_kernel(got_ref, out_ref):
    halves_of = [got_ref[0, :16], got_ref[1, :16]]
    gram = got_ref[0, 16:]
    for peer in range(1, 16):
        gram = gram + got_ref[peer, 16:]
        if peer > 1:
            halves_of[peer % 2] = halves_of[peer % 2] + got_ref[peer, :16]
    for peer in range(16):
        out_ref[peer, :16] = halves_of[0]
        out_ref[peer, 16:32] = halves_of[1]
        out_ref[peer, 32:] = gram


def sum_copies(got):
    return pl.pallas_call(
        sum_kernel,
        out_shape=jax.ShapeDtypeStruct((16, 56, 128), f32),
        compiler_params=params(16),
        cost_estimate=cost(1e6, MIB),
        name="sum_copies",
    )(got)


def finish_kernel(
    pixels,
    channels,
    got_ref,
    weight_in,
    blend_in,
    y_in,
    wave_out,
    mixed_out,
    weight_ref,
    blend_ref,
    wave_ref,
    y_ref,
    mixed_ref,
    in_sems,
    out_sems,
):
    coming = [
        pltpu.make_async_copy(weight_in, weight_ref, in_sems.at[5]),
        pltpu.make_async_copy(y_in.at[:2], y_ref, in_sems.at[4]),
    ]
    arrived = [
        pltpu.make_async_copy(blend_in.at[band], blend_ref.at[band], in_sems.at[band])
        for band in range(4)
    ]
    for copy in coming + arrived:
        copy.start()
    going = []

    def wave(band):
        if band == 0:
            coming[0].wait()
        arrived[band].wait()
        for part in range(4):
            rows = slice(8 * part, 8 * part + 8)
            for q in range(4):
                lanes = slice(128 * q, 128 * q + 128)
                energy = got_ref[4 * band + part, 8 * q : 8 * q + 8, :]
                ratio = jnp.sqrt(energy * (1.0 / channels)) / weight_ref[band, rows, lanes]
                scale = 1.0 / jnp.maximum(1.0, ratio)
                wave_ref[band, :, rows, lanes] = blend_ref[band, :, rows, lanes] * scale[None]
        copy = pltpu.make_async_copy(wave_ref.at[band], wave_out.at[band], out_sems.at[band])
        copy.start()
        going.append(copy)

    size = 256
    rows = lax.broadcasted_iota(jnp.int32, (size, size), 0)
    cols = lax.broadcasted_iota(jnp.int32, (size, size), 1)
    blocks = []
    for peer in range(16):
        ninth = jnp.concatenate([got_ref[peer, 48:, :], jnp.zeros((8, 128), f32)], axis=0)
        second = jnp.concatenate([jnp.zeros((8, 128), f32), pltpu.roll(got_ref[peer, 48:, :], 112, 1)], axis=0)
        ninth = ninth + second
        block = jnp.concatenate([got_ref[peer, 32:48, :], ninth], axis=1)
        blocks.append(pltpu.roll(block, 16 * peer, 1) if peer else block)
    half = jnp.concatenate(blocks, axis=0)
    known = (cols // 16 - rows // 16) % 16 < 9
    gram = jnp.where(known, half, half.T)
    shifted = (rows == cols).astype(f32) + gram * (1.0 / pixels)
    frob = jnp.sqrt(jnp.sum(shifted * shifted, keepdims=True))

    def middle_of(product):
        return jnp.where(rows == cols, 1.5, 0.0) - 0.5 * product

    product = shifted / frob
    middle = middle_of(product)
    inverse = middle
    for turn in range(1, NSTEP):
        mh, ml = halves(middle)
        if turn == 1:
            first = mm3_right(product, mh, ml)
        else:
            both = mm3_right(jnp.concatenate([product, inverse], axis=0), mh, ml)
            first, inverse = both[:size], both[size:]
        if turn > 2:
            wave(2 * turn - 6)
            wave(2 * turn - 5)
        product = mm3_right(first, mh, ml)
        middle = middle_of(product)
    mh, ml = halves(middle)
    mh, ml = halves(mm3_right(inverse, mh, ml) * lax.rsqrt(frob))
    coming[1].wait()
    for block in range(4):
        span = pl.ds(256 * block, 256)
        yh = y_ref[0, span, :]
        mixed_ref[span, :] = mm(yh, mh) + (mm(yh, ml) + mm(y_ref[1, span, :], mh))
        copy = pltpu.make_async_copy(mixed_ref.at[span], mixed_out.at[span], out_sems.at[4 + block])
        copy.start()
        going.append(copy)
    for copy in going:
        copy.wait()


def finish(got, weights, blended, y, pixels, channels):
    shape = (4, 16, 32, 512)
    hbm = pl.BlockSpec(memory_space=pl.ANY)
    return pl.pallas_call(
        lambda *refs: finish_kernel(pixels, channels, *refs),
        in_specs=[pl.BlockSpec(memory_space=pltpu.VMEM)] + [hbm] * 3,
        out_specs=(hbm, hbm),
        out_shape=(
            jax.ShapeDtypeStruct(shape, f32),
            jax.ShapeDtypeStruct((1024, 256), f32),
        ),
        scratch_shapes=[
            pltpu.VMEM(weights.shape, f32),
            pltpu.VMEM(shape, f32),
            pltpu.VMEM(shape, f32),
            pltpu.VMEM((2, 1024, 256), bf16),
            pltpu.VMEM((1024, 256), f32),
            pltpu.SemaphoreType.DMA((6,)),
            pltpu.SemaphoreType.DMA((8,)),
        ],
        compiler_params=params(40),
        cost_estimate=cost(2e9, 8 * MIB),
        name="finish",
    )(got, weights, blended, y)


def filter_tables(first, last):
    both = (low_taps, high_taps)
    count = last - first
    down = np.zeros((2, 4, count, 4, count + 8))
    across = np.zeros((256, 2, 128))
    for which, taps in enumerate(both):
        for m, tap in enumerate(taps):
            for row in range(count):
                for ch in range(4):
                    down[which, ch, row, ch, 8 + row - m] = tap
            for col in range(128):
                across[128 + col - m, which, col] = 0.5 * tap
    down = np.stack(host_halves(down.reshape(8 * count, 4 * count + 32)))
    return down, np.concatenate(host_halves(across.reshape(256, 256)))


def copy_in(source, target, sem):
    copy = pltpu.make_async_copy(source, target, sem)
    copy.start()
    return copy


def blend_group(pieces, four, first, down_ref, across_ref, dual_ref, blend_ref, energy_ref):
    count = dual_ref.shape[2]
    eh, el = halves(jnp.concatenate(pieces, axis=0))
    dh, dl = down_ref[0], down_ref[1]
    filtered = mm(dh, eh) + (mm(dh, el) + mm(dl, eh))
    vh, vl = halves(filtered)
    for j in range(4):
        if j:
            lanes = slice(128 * j - 128, 128 * j + 128)
            ah, al = across_ref[:256, :], across_ref[256:, :]
        else:
            lanes = slice(0, 128)
            ah, al = across_ref[128:256, :], across_ref[384:, :]
        done = mm(vh[:, lanes], ah) + (mm(vl[:, lanes], ah) + mm(vh[:, lanes], al))
        here = slice(128 * j, 128 * j + 128)
        place = slice(8 * (j % 2), 8 * (j % 2) + 8)
        for band in range(4):
            part = done[4 * count * (band // 2) : 4 * count * (band // 2) + 4 * count]
            part = part[:, 128 * (band % 2) : 128 * (band % 2) + 128].reshape(4, count, 128)
            blended = dual_ref[band, four, :, here] + part
            blend_ref[band, four, :, here] = blended
            squares = jnp.sum(blended * blended, axis=0)
            for strip in range(count // 8):
                energy_ref[j // 2, 4 * band + first // 8 + strip, place, :] += squares[
                    8 * strip : 8 * strip + 8
                ]


def inner_kernel(
    sky_in,
    dual_in,
    down_in,
    across_in,
    blend_out,
    energy_out,
    sky_ref,
    dual_ref,
    down_ref,
    across_ref,
    blend_ref,
    energy_ref,
    in_sems,
    out_sems,
):
    fours = [slice(4 * k, 4 * k + 4) for k in range(4)]
    down = copy_in(down_in, down_ref, in_sems.at[0])
    sky, dual = [], []
    for k, four in enumerate(fours):
        sky.append(copy_in(sky_in.at[four], sky_ref.at[four], in_sems.at[2 + k]))
        if k == 0:
            across = copy_in(across_in, across_ref, in_sems.at[1])
        dual.append(copy_in(dual_in.at[:, four, 8:], dual_ref.at[:, four], in_sems.at[6 + k]))
    energy_ref[...] = jnp.zeros_like(energy_ref)
    down.wait()
    going = []
    for k, four in enumerate(fours):
        sky[k].wait()
        if k == 0:
            across.wait()
        dual[k].wait()
        pieces = [sky_ref[c] for c in range(4 * k, 4 * k + 4)]
        blend_group(pieces, four, 8, down_ref, across_ref, dual_ref, blend_ref, energy_ref)
        going.append(copy_in(blend_ref.at[:, four], blend_out.at[:4, four, 8:], out_sems.at[k]))
    going.append(copy_in(energy_ref, energy_out, out_sems.at[4]))
    for copy in going:
        copy.wait()


def outer_kernel(
    margins_ref,
    sky_in,
    rim_in,
    dual_in,
    down_in,
    across_in,
    energy_in,
    blend_in,
    blend_out,
    kept_out,
    sent_out,
    sky_ref,
    rim_ref,
    dual_ref,
    down_ref,
    across_ref,
    blend_ref,
    energy_ref,
    in_sems,
    out_sems,
):
    margin = margins_ref[lax.axis_index("facet")]
    half = lax.axis_index("chan") % 2
    row = lax.broadcasted_iota(jnp.int32, (8, 512), 0)
    kept = row >= 8 - margin
    coming = [
        copy_in(source, target, in_sems.at[k])
        for k, (source, target) in enumerate(
            (
                (rim_in, rim_ref),
                (sky_in.at[:, :8], sky_ref),
                (down_in, down_ref),
                (across_in, across_ref),
                (energy_in, energy_ref),
                (dual_in.at[:, :, :8], dual_ref),
            )
        )
    ]
    for copy in coming:
        copy.wait()
    going = []
    for k in range(4):
        four = slice(4 * k, 4 * k + 4)
        pieces = []
        for c in range(4 * k, 4 * k + 4):
            pieces += [jnp.where(kept, rim_ref[c], 0.0), sky_ref[c]]
        blend_group(pieces, four, 0, down_ref, across_ref, dual_ref, blend_ref, energy_ref)
        going.append(copy_in(blend_ref.at[:, four], blend_out.at[:4, four, :8], out_sems.at[k]))
    for number, (which, target) in enumerate(((1 - half, sent_out), (half, kept_out))):
        going.append(copy_in(energy_ref.at[which], target, out_sems.at[4 + number]))
    for copy in going:
        copy.wait()


def blend_inner(sky, dual):
    down, across = (jnp.asarray(t) for t in filter_tables(8, 32))
    hbm = pl.BlockSpec(memory_space=pl.ANY)
    return pl.pallas_call(
        inner_kernel,
        in_specs=[hbm] * 4,
        out_specs=(hbm, hbm),
        out_shape=(
            jax.ShapeDtypeStruct((ROOM, 16, 32, 512), f32),
            jax.ShapeDtypeStruct((2, 16, 16, 128), f32),
        ),
        scratch_shapes=[
            pltpu.VMEM(sky.shape, f32),
            pltpu.VMEM((4, 16, 24, 512), f32),
            pltpu.VMEM(down.shape, bf16),
            pltpu.VMEM(across.shape, bf16),
            pltpu.VMEM((4, 16, 24, 512), f32),
            pltpu.VMEM((2, 16, 16, 128), f32),
            pltpu.SemaphoreType.DMA((10,)),
            pltpu.SemaphoreType.DMA((5,)),
        ],
        compiler_params=params(60),
        cost_estimate=cost(2e9, 8 * MIB),
        name="blend_inner",
    )(sky, dual, down, across)


def blend_outer(margins, sky, rim, dual, energy, blended):
    down, across = (jnp.asarray(t) for t in filter_tables(0, 8))
    hbm = pl.BlockSpec(memory_space=pl.ANY)
    return pl.pallas_call(
        outer_kernel,
        in_specs=[pl.BlockSpec(memory_space=pltpu.SMEM)] + [hbm] * 7,
        out_specs=(hbm, hbm, hbm),
        out_shape=(
            jax.ShapeDtypeStruct(blended.shape, f32),
            jax.ShapeDtypeStruct((16, 16, 128), f32),
            jax.ShapeDtypeStruct((16, 16, 128), f32),
        ),
        input_output_aliases={7: 0},
        scratch_shapes=[
            pltpu.VMEM((16, 8, 512), f32),
            pltpu.VMEM((16, 8, 512), f32),
            pltpu.VMEM((4, 16, 8, 512), f32),
            pltpu.VMEM(down.shape, bf16),
            pltpu.VMEM(across.shape, bf16),
            pltpu.VMEM((4, 16, 8, 512), f32),
            pltpu.VMEM((2, 16, 16, 128), f32),
            pltpu.SemaphoreType.DMA((6,)),
            pltpu.SemaphoreType.DMA((6,)),
        ],
        compiler_params=params(60),
        cost_estimate=cost(1e9, 4 * MIB),
        name="blend_outer",
    )(margins, sky, rim, dual, down, across, energy, blended)


def degrid_tables(side):
    column = np.arange(side, dtype=np.int64)[None, :]
    kx = np.arange(KT, dtype=np.int64)[:, None]
    tile = np.arange(side // KT, dtype=np.int64)[:, None]
    inner = (kx * column % side) * (2.0 * np.pi / side)
    outer = (KT * tile * column % side) * (2.0 * np.pi / side)
    columns = np.concatenate([np.cos(inner), np.sin(inner), np.cos(outer), np.sin(outer)])
    ky, row = np.arange(16)[:, None], np.arange(32)[None, :]
    turn = ky * row * (2.0 * np.pi / side)
    whole = np.zeros((16, 4, 2, 2, 4, 32))
    for ch in range(4):
        whole[:, ch, 0, 0, ch, :] = np.cos(turn)
        whole[:, ch, 0, 1, ch, :] = np.sin(turn)
        whole[:, ch, 1, 0, ch, :] = -np.sin(turn)
        whole[:, ch, 1, 1, ch, :] = np.cos(turn)
    rows = np.concatenate(host_halves(whole.reshape(128, 256)))
    shift = np.arange(32)[:, None] * np.arange(32)[None, :] * (2.0 * np.pi / 32)
    shift = np.concatenate(host_halves(np.concatenate([np.cos(shift), np.sin(shift)])))
    turn = np.arange(16) * (2.0 * np.pi / 16)
    turn = np.stack([np.cos(turn), np.sin(turn)]).astype(np.float32)
    return columns.astype(np.float32), rows, shift, turn


def channel_at(place):
    b0, b3, b1, b2 = ((place >> k) & 1 for k in (3, 2, 1, 0))
    return b0 + 2 * b1 + 4 * b2 + 8 * b3


def degrid_kernel(
    tile_ref,
    turn_ref,
    sky_ref,
    shift_ref,
    column_ref,
    row_ref,
    weight_in,
    out_ref,
    xh_ref,
    xl_ref,
    table_ref,
    t_ref,
    u_ref,
    weight_ref,
    sem,
):
    coming = pltpu.make_async_copy(weight_in, weight_ref, sem.at[0])
    coming.start()
    facet = lax.axis_index("facet")
    inner_cos, inner_sin = column_ref[:KT, :], column_ref[KT : 2 * KT, :]
    block = lax.broadcasted_iota(jnp.int32, (8, 512), 1) // KT
    ty = jnp.zeros((8, 512), jnp.int32)
    for b in range(32):
        tile = tile_ref[0, b]
        ty = jnp.where(block == b, tile // 32, ty)
        outer_cos = column_ref[pl.ds(2 * KT + tile % 32, 1), :]
        outer_sin = column_ref[pl.ds(2 * KT + 32 + tile % 32, 1), :]
        rows = slice(KT * b, KT * b + KT)
        both = (
            inner_cos * outer_cos - inner_sin * outer_sin,
            inner_sin * outer_cos + inner_cos * outer_sin,
        )
        for k, values in enumerate(both):
            upper, lower = halves(values)
            table_ref[2 * k, rows, :] = upper
            table_ref[2 * k + 1, rows, :] = lower
    for place in range(16):
        xh, xl = halves(sky_ref[channel_at(place)])
        xh_ref[32 * place : 32 * place + 32, :] = xh
        xl_ref[32 * place : 32 * place + 32, :] = xl
    wanted = lax.broadcasted_iota(jnp.int32, (32, 512), 0) == ty[:1, :]
    phase = mm(shift_ref[...], wanted.astype(f32).astype(bf16))
    phase = (phase[:64] + phase[64:]).reshape(2, 32, 512)
    cos_h, cos_l, sin_h, sin_l = (table_ref[k] for k in range(4))
    row_h, row_l = row_ref[:128, :], row_ref[128:, :]
    for half in range(4):
        rows = slice(128 * half, 128 * half + 128)
        xh, xl = xh_ref[rows, :], xl_ref[rows, :]
        gc = mm_t(xh, cos_h) + (mm_t(xl, cos_h) + mm_t(xh, cos_l))
        gs = mm_t(xh, sin_h) + (mm_t(xl, sin_h) + mm_t(xh, sin_l))
        gc, gs = gc.reshape(4, 32, 512), gs.reshape(4, 32, 512)
        pc, ps = phase[0][None], phase[1][None]
        pre = (gc * pc - gs * ps).reshape(128, 512)
        pim = (-(gs * pc + gc * ps)).reshape(128, 512)
        both_h, both_l = halves(jnp.concatenate([pre, pim], axis=0))
        t_ref[half] = mm(row_h, both_h) + (mm(row_l, both_h) + mm(row_h, both_l))
    even = lax.broadcasted_iota(jnp.int32, (8, 128), 0) % 2 == 0
    coming.wait()
    for quarter in range(4):
        for four in range(4):
            for high in range(2):
                parts = []
                for low in range(8):
                    ky = 8 * high + low
                    part = t_ref[four, 8 * ky : 8 * ky + 8, 128 * quarter : 128 * quarter + 128]
                    other = jnp.where(even, pltpu.roll(part, 7, 0), -pltpu.roll(part, 1, 0))
                    spot = ky * facet % 16
                    parts.append(part * turn_ref[0, spot] + other * turn_ref[1, spot])
                for b, done in enumerate(swap_chunks(parts, 16)):
                    u_ref[32 * b + 8 * four : 32 * b + 8 * four + 8, 128 * high : 128 * high + 128] = done
        uh, ul = halves(u_ref[...])
        rows = slice(256 * quarter, 256 * quarter + 256)
        sums = []
        for part in range(2):
            weights = weight_ref[rows, 256 * part : 256 * part + 256]
            sums.append(mm_t(uh, weights) + mm_t(ul, weights))
        lane = lax.broadcasted_iota(jnp.int32, (32, 256), 1)
        row = lax.broadcasted_iota(jnp.int32, (32, 256), 0)
        first = jnp.zeros((32, 256), f32)
        second = jnp.zeros((32, 256), f32)
        for b in range(8):
            mine = lane // 32 == b
            first = jnp.where(mine, sums[0][32 * b : 32 * b + 32, :], first)
            second = jnp.where(mine, sums[1][32 * b : 32 * b + 32, :], second)
        other = jnp.where(row % 2 == 0, -pltpu.roll(second, 31, 0), pltpu.roll(second, 1, 0))
        out_ref[:, 256 * quarter : 256 * quarter + 256] = (first + other) * (1.0 / 512.0)


def degrid(sky, weights, tile_ids):
    columns, rows, shift, turn = (jnp.asarray(t) for t in degrid_tables(sky.shape[-1]))
    smem = pl.BlockSpec(memory_space=pltpu.SMEM)
    vmem = pl.BlockSpec(memory_space=pltpu.VMEM)
    return pl.pallas_call(
        degrid_kernel,
        in_specs=[smem, smem] + [vmem] * 4 + [pl.BlockSpec(memory_space=pl.ANY)],
        out_specs=vmem,
        out_shape=jax.ShapeDtypeStruct((32, 1024), f32),
        scratch_shapes=[
            pltpu.VMEM((512, 512), bf16),
            pltpu.VMEM((512, 512), bf16),
            pltpu.VMEM((4, 512, 512), bf16),
            pltpu.VMEM((4, 128, 512), f32),
            pltpu.VMEM((256, 256), f32),
            pltpu.VMEM((1024, 512), bf16),
            pltpu.SemaphoreType.DMA((1,)),
        ],
        compiler_params=params(60),
        cost_estimate=cost(3e9, 6 * MIB),
        name="degrid",
    )(tile_ids, turn, sky, shift, columns, rows, weights)


def split_kernel(values_ref, sent_ref, kept_ref):
    core = lax.axis_index("facet") % 2
    sent_ref[...] = values_ref[pl.ds(pl.multiple_of(16 * (1 - core), 16), 16), :]
    kept_ref[...] = values_ref[pl.ds(pl.multiple_of(16 * core, 16), 16), :]


def split(values):
    return pl.pallas_call(
        split_kernel,
        out_shape=(jax.ShapeDtypeStruct((16, 1024), f32),) * 2,
        compiler_params=params(16),
        cost_estimate=cost(1e6, 16 * MIB),
        name="split",
    )(values)


def data_step(data_dual, forward, visibilities, radius_scale):
    moved = data_dual + forward
    residual = 2.0 * moved - visibilities
    distance = jnp.sqrt(jnp.sum(residual * residual, axis=(1, 2)) + 1e-06)
    radius = radius_scale * math.sqrt(2.0 * visibilities.shape[2])
    shrunk = jnp.minimum(1.0, radius / distance)
    return moved - 0.5 * (visibilities + residual * shrunk[:, None, None])


def trade(values, axis):
    return lax.all_to_all(values, axis, 0, 0, tiled=True)


def facet_pairs(bit):
    return [(i, i ^ (1 << bit)) for i in range(lax.axis_size("facet"))]


def halving_sum(values, bits):
    me = lax.axis_index("facet")
    for bit in bits:
        values = values.reshape(2, values.shape[0] // 2, values.shape[1])
        mine = (me >> bit) & 1
        sent = lax.dynamic_index_in_dim(values, 1 - mine, 0, keepdims=False)
        kept = lax.dynamic_index_in_dim(values, mine, 0, keepdims=False)
        values = kept + lax.ppermute(sent, "facet", facet_pairs(bit))
    return values


def per_device(
    sky_image,
    margins,
    wavelet_dual,
    sparsity_weights,
    lowrank_dual,
    kernel_weights,
    tile_index,
    data_dual,
    visibilities,
    radius_scale,
):
    facet_rows, image_side = sky_image.shape[1:]
    channels = lowrank_dual.shape[0]
    devices = lax.axis_size("facet")

    packed, rim = pack_sky(sky_image)
    packed, sky = lax.optimization_barrier((packed, sky_image))
    got = trade(packed, "chan").reshape(2048, 128)
    rim = lax.ppermute(rim, "facet", [(i, i + 1) for i in range(devices - 1)])
    blended, energy = blend_inner(sky, wavelet_dual)
    blended, kept, sent = blend_outer(margins, sky, rim, wavelet_dual, energy, blended)
    other = lax.ppermute(sent, "chan", [(i, i ^ 1) for i in range(lax.axis_size("chan"))])
    sky, kept = lax.optimization_barrier((sky, kept))
    forward_part = degrid(sky, kernel_weights.reshape(1024, 512), tile_index)
    sent, mine = split(forward_part)
    forward = mine + lax.ppermute(sent, "facet", facet_pairs(0))
    kept, forward = lax.optimization_barrier((kept, forward))

    dual = jnp.transpose(lowrank_dual, (1, 2, 0)).reshape(4, 8, 32, 256)
    y, part = gram_part(got, dual, kept, other)
    part, forward = lax.optimization_barrier((part, forward))
    forward = halving_sum(forward, (3,))
    reduced, forward = lax.optimization_barrier((trade(part, "chan"), forward))
    forward = halving_sum(forward, (1, 2))[None]
    data_next = data_step(data_dual, forward, visibilities, radius_scale)
    total = trade(sum_copies(reduced), "chan")
    wavelet_next, mixed = finish(
        total, sparsity_weights, blended, y.reshape(2 * ROOM, 1024, 256), facet_rows * image_side, channels
    )
    lowrank_next = jnp.transpose(mixed.reshape(32, 32, 256), (2, 0, 1))
    return (wavelet_next, lowrank_next, data_next)


def solution(mesh):
    in_specs = (
        P("chan", "facet", None),
        P(),
        P(None, "chan", "facet", None),
        P(None, "facet", None),
        P(None, "facet", "chan"),
        P("chan", None, None, None),
        P("chan", None),
        P(("chan", "facet"), None, None),
        P(("chan", "facet"), None, None),
        P(("chan", "facet")),
    )
    out_specs = (
        P(None, "chan", "facet", None),
        P(None, "facet", "chan"),
        P(("chan", "facet"), None, None),
    )
    return jax.shard_map(
        per_device, mesh=mesh, in_specs=in_specs, out_specs=out_specs, check_vma=False
    )
```

```python
import math

import jax
import jax.numpy as jnp
import ml_dtypes
import numpy as np
from jax import lax
from jax.experimental import pallas as pl
from jax.experimental.pallas import tpu as pltpu
from jax.sharding import PartitionSpec as P

NSTEP = 5
KT = 16
MIB = 1 << 20
ROOM = 24

low_taps = (
    -0.010597401784997278,
    0.032883011666982945,
    0.030841381835986965,
    -0.18703481171888114,
    -0.02798376941698385,
    0.6308807679295904,
    0.7148465705525415,
    0.23037781330885523,
)
high_taps = tuple(((-1.0) ** offset * low_taps[7 - offset] for offset in range(8)))
f32 = jnp.float32
bf16 = jnp.bfloat16


def params(mib):
    return pltpu.CompilerParams(vmem_limit_bytes=int(mib * MIB))


def cost(flops, nbytes):
    return pl.CostEstimate(flops=int(flops), bytes_accessed=int(nbytes), transcendentals=0)


def halves(values):
    upper = values.astype(bf16)
    return upper, (values - upper.astype(f32)).astype(bf16)


def host_halves(values):
    values = values.astype(np.float32)
    upper = values.astype(ml_dtypes.bfloat16)
    return upper, (values - upper.astype(np.float32)).astype(ml_dtypes.bfloat16)


def mm(a, b):
    return jnp.dot(a, b, preferred_element_type=f32)


def mm_t(a, b):
    return lax.dot_general(a, b, (((1,), (1,)), ((), ())), preferred_element_type=f32)


def mm3_right(a, bh, bl):
    ah, al = halves(a)
    return mm(ah, bh) + (mm(ah, bl) + mm(al, bh))


def swap_chunks(parts, width):
    count = len(parts)
    lane = lax.broadcasted_iota(jnp.int32, parts[0].shape, len(parts[0].shape) - 1)
    axis = len(parts[0].shape) - 1
    step = count // 2
    while step:
        span = step * width
        first = (lane // span) % 2 == 0
        out = list(parts)
        for a in range(count):
            if a & step:
                continue
            b = a | step
            out[a] = jnp.where(first, parts[a], pltpu.roll(parts[b], span, axis))
            out[b] = jnp.where(first, pltpu.roll(parts[a], 128 - span, axis), parts[b])
        parts = out
        step //= 2
    return parts


def pack_kernel(sky_in, packed_out, rim_out, sky_ref, packed_ref, in_sems, out_sems):
    fours = [slice(4 * k, 4 * k + 4) for k in range(4)]
    coming = [
        pltpu.make_async_copy(sky_in.at[four], sky_ref.at[four], in_sems.at[k])
        for k, four in enumerate(fours)
    ]
    going = [
        pltpu.make_async_copy(packed_ref.at[:, four], packed_out.at[:, four], out_sems.at[k])
        for k, four in enumerate(fours)
    ]
    going.append(pltpu.make_async_copy(sky_ref.at[:, 24:, :], rim_out, out_sems.at[4]))
    for copy in coming:
        copy.start()
    for k, four in enumerate(fours):
        coming[k].wait()
        for quarter in range(4):
            lanes = slice(128 * quarter, 128 * quarter + 128)
            parts = [sky_ref[four, 8 * j : 8 * j + 8, lanes] for j in range(4)]
            for s, done in enumerate(swap_chunks(parts, 32)):
                packed_ref[4 * quarter + s, four] = done
        going[k].start()
    going[4].start()
    for copy in going:
        copy.wait()


def pack_sky(sky):
    hbm = pl.BlockSpec(memory_space=pl.ANY)
    return pl.pallas_call(
        pack_kernel,
        in_specs=[hbm],
        out_specs=(hbm, hbm),
        out_shape=(
            jax.ShapeDtypeStruct((16, 16, 8, 128), f32),
            jax.ShapeDtypeStruct((16, 8, 512), f32),
        ),
        scratch_shapes=[
            pltpu.VMEM((16, 32, 512), f32),
            pltpu.VMEM((16, 16, 8, 128), f32),
            pltpu.SemaphoreType.DMA((4,)),
            pltpu.SemaphoreType.DMA((5,)),
        ],
        compiler_params=params(60),
        cost_estimate=cost(3e6, 2 * MIB),
        name="pack_sky",
    )(sky)


def turn_rows(block, back):
    row = lax.broadcasted_iota(jnp.int32, block.shape, 0)
    for bit in (1, 2, 4, 8):
        turned = pltpu.roll(block, bit if back else 256 - bit, 1)
        block = jnp.where((row // bit) % 2 == 1, turned, block)
    return block


def gram_kernel(
    got_ref, dual_ref, blend_in, other_ref, y_out, part_out, y_ref, kept_ref, sum_ref, gram_ref, sems
):
    kept = copy_in(blend_in.at[4, :, :16, :128], kept_ref, sems.at[10])
    total = jnp.zeros((256, 256), f32)
    cross = jnp.zeros((256, 256), f32)
    held, copies = [], []
    for low in range(8):
        seen = got_ref[pl.ds(low, 256, stride=8), :].T
        right = dual_ref[:, low].reshape(128, 256) + 0.5 * seen
        rh, rl = halves(right)
        y_ref[0, :, low] = rh.reshape(4, 32, 256)
        y_ref[1, :, low] = rl.reshape(4, 32, 256)
        copies.append(pltpu.make_async_copy(y_ref.at[:, :, low], y_out.at[:2, :, low], sems.at[low]))
        copies[-1].start()
        held.append((rh, rl))
        if low % 4 == 3:
            rh = jnp.concatenate([upper for upper, _ in held], axis=0)
            rl = jnp.concatenate([lower for _, lower in held], axis=0)
            held = []
            lh = rh.T
            total = total + mm(lh, rh)
            cross = cross + mm(lh, rl)
    total = total + (cross + cross.T)
    kept.wait()
    sum_ref[...] = kept_ref[...] + other_ref[...]
    copies.append(copy_in(sum_ref, part_out.at[:, :16], sems.at[8]))
    row = lax.broadcasted_iota(jnp.int32, (128, 128), 0)
    lane = lax.broadcasted_iota(jnp.int32, (128, 128), 1)
    far = jnp.sum(jnp.where(row == lane, total[:128, 128:], 0.0), axis=0, keepdims=True)
    gram_ref[:, 16:, :] = jnp.broadcast_to(far[None], (16, 8, 128))
    for peer in range(16):
        turned = total[16 * peer : 16 * peer + 16, :]
        if peer:
            turned = pltpu.roll(turned, 256 - 16 * peer, 1)
        gram_ref[peer, :16, :] = turn_rows(turned, False)[:, :128]
    copies.append(pltpu.make_async_copy(gram_ref, part_out.at[:, 16:], sems.at[9]))
    copies[-1].start()
    for copy in copies:
        copy.wait()


def gram_part(got, dual, blended, other):
    vmem = pl.BlockSpec(memory_space=pltpu.VMEM)
    hbm = pl.BlockSpec(memory_space=pl.ANY)
    return pl.pallas_call(
        gram_kernel,
        in_specs=[vmem, vmem, hbm, vmem],
        out_specs=(hbm, hbm),
        out_shape=(
            jax.ShapeDtypeStruct((2 * ROOM, 4, 8, 32, 256), bf16),
            jax.ShapeDtypeStruct((16, 40, 128), f32),
        ),
        scratch_shapes=[
            pltpu.VMEM((2, 4, 8, 32, 256), bf16),
            pltpu.VMEM((16, 16, 128), f32),
            pltpu.VMEM((16, 16, 128), f32),
            pltpu.VMEM((16, 24, 128), f32),
            pltpu.SemaphoreType.DMA((11,)),
        ],
        compiler_params=params(40),
        cost_estimate=cost(4e8, 3 * MIB),
        name="gram_part",
    )(got, dual, blended, other)


def sum_kernel(got_ref, out_ref, far_ref):
    halves_of = [got_ref[0, :16], got_ref[1, :16]]
    gram = got_ref[0, 16:]
    for peer in range(1, 16):
        gram = gram + got_ref[peer, 16:]
        if peer > 1:
            halves_of[peer % 2] = halves_of[peer % 2] + got_ref[peer, :16]
    far_ref[...] = gram[16:]
    for peer in range(16):
        out_ref[peer, :16] = halves_of[0]
        out_ref[peer, 16:32] = halves_of[1]
        out_ref[peer, 32:] = gram[:16]


def sum_copies(got):
    return pl.pallas_call(
        sum_kernel,
        out_shape=(
            jax.ShapeDtypeStruct((16, 48, 128), f32),
            jax.ShapeDtypeStruct((8, 128), f32),
        ),
        compiler_params=params(16),
        cost_estimate=cost(1e6, MIB),
        name="sum_copies",
    )(got)


def finish_kernel(
    pixels,
    channels,
    got_ref,
    far_ref,
    weight_in,
    blend_in,
    y_in,
    wave_out,
    mixed_out,
    weight_ref,
    blend_ref,
    wave_ref,
    y_ref,
    mixed_ref,
    in_sems,
    out_sems,
):
    coming = [
        pltpu.make_async_copy(weight_in, weight_ref, in_sems.at[5]),
        pltpu.make_async_copy(y_in.at[:2], y_ref, in_sems.at[4]),
    ]
    arrived = [
        pltpu.make_async_copy(blend_in.at[band], blend_ref.at[band], in_sems.at[band])
        for band in range(4)
    ]
    for copy in coming + arrived:
        copy.start()
    going = []

    def wave(band):
        if band == 0:
            coming[0].wait()
        arrived[band].wait()
        for part in range(4):
            rows = slice(8 * part, 8 * part + 8)
            for q in range(4):
                lanes = slice(128 * q, 128 * q + 128)
                energy = got_ref[4 * band + part, 8 * q : 8 * q + 8, :]
                ratio = jnp.sqrt(energy * (1.0 / channels)) / weight_ref[band, rows, lanes]
                scale = 1.0 / jnp.maximum(1.0, ratio)
                wave_ref[band, :, rows, lanes] = blend_ref[band, :, rows, lanes] * scale[None]
        copy = pltpu.make_async_copy(wave_ref.at[band], wave_out.at[band], out_sems.at[band])
        copy.start()
        going.append(copy)

    size = 256
    rows = lax.broadcasted_iota(jnp.int32, (size, size), 0)
    cols = lax.broadcasted_iota(jnp.int32, (size, size), 1)
    blocks = []
    nothing = jnp.zeros((16, 128), f32)
    for peer in range(16):
        block = turn_rows(jnp.concatenate([got_ref[peer, 32:48, :], nothing], axis=1), True)
        blocks.append(pltpu.roll(block, 16 * peer, 1) if peer else block)
    half = jnp.concatenate(blocks, axis=0)
    far = far_ref[:1, :]
    apart = (cols - rows) % 256
    gram = jnp.where(apart < 128, half, half.T)
    gram = jnp.where(apart == 128, jnp.concatenate([far, far], axis=1), gram)
    shifted = (rows == cols).astype(f32) + gram * (1.0 / pixels)
    frob = jnp.sqrt(jnp.sum(shifted * shifted, keepdims=True))

    def middle_of(product):
        return jnp.where(rows == cols, 1.5, 0.0) - 0.5 * product

    product = shifted / frob
    middle = middle_of(product)
    inverse = middle
    for turn in range(1, NSTEP):
        mh, ml = halves(middle)
        if turn == 1:
            first = mm3_right(product, mh, ml)
        else:
            both = mm3_right(jnp.concatenate([product, inverse], axis=0), mh, ml)
            first, inverse = both[:size], both[size:]
        if turn > 2:
            wave(2 * turn - 6)
            wave(2 * turn - 5)
        product = mm3_right(first, mh, ml)
        middle = middle_of(product)
    mh, ml = halves(middle)
    mh, ml = halves(mm3_right(inverse, mh, ml) * lax.rsqrt(frob))
    coming[1].wait()
    for block in range(4):
        span = pl.ds(256 * block, 256)
        yh = y_ref[0, span, :]
        mixed_ref[span, :] = mm(yh, mh) + (mm(yh, ml) + mm(y_ref[1, span, :], mh))
        copy = pltpu.make_async_copy(mixed_ref.at[span], mixed_out.at[span], out_sems.at[4 + block])
        copy.start()
        going.append(copy)
    for copy in going:
        copy.wait()


def finish(got, far, weights, blended, y, pixels, channels):
    shape = (4, 16, 32, 512)
    hbm = pl.BlockSpec(memory_space=pl.ANY)
    return pl.pallas_call(
        lambda *refs: finish_kernel(pixels, channels, *refs),
        in_specs=[pl.BlockSpec(memory_space=pltpu.VMEM)] * 2 + [hbm] * 3,
        out_specs=(hbm, hbm),
        out_shape=(
            jax.ShapeDtypeStruct(shape, f32),
            jax.ShapeDtypeStruct((1024, 256), f32),
        ),
        scratch_shapes=[
            pltpu.VMEM(weights.shape, f32),
            pltpu.VMEM(shape, f32),
            pltpu.VMEM(shape, f32),
            pltpu.VMEM((2, 1024, 256), bf16),
            pltpu.VMEM((1024, 256), f32),
            pltpu.SemaphoreType.DMA((6,)),
            pltpu.SemaphoreType.DMA((8,)),
        ],
        compiler_params=params(40),
        cost_estimate=cost(2e9, 8 * MIB),
        name="finish",
    )(got, far, weights, blended, y)


def filter_tables(first, last):
    both = (low_taps, high_taps)
    count = last - first
    down = np.zeros((2, 4, count, 4, count + 8))
    across = np.zeros((256, 2, 128))
    for which, taps in enumerate(both):
        for m, tap in enumerate(taps):
            for row in range(count):
                for ch in range(4):
                    down[which, ch, row, ch, 8 + row - m] = tap
            for col in range(128):
                across[128 + col - m, which, col] = 0.5 * tap
    down = np.stack(host_halves(down.reshape(8 * count, 4 * count + 32)))
    return down, np.concatenate(host_halves(across.reshape(256, 256)))


def copy_in(source, target, sem):
    copy = pltpu.make_async_copy(source, target, sem)
    copy.start()
    return copy


def blend_group(pieces, four, first, down_ref, across_ref, dual_ref, blend_ref, energy_ref):
    count = dual_ref.shape[2]
    eh, el = halves(jnp.concatenate(pieces, axis=0))
    dh, dl = down_ref[0], down_ref[1]
    filtered = mm(dh, eh) + (mm(dh, el) + mm(dl, eh))
    vh, vl = halves(filtered)
    for j in range(4):
        if j:
            lanes = slice(128 * j - 128, 128 * j + 128)
            ah, al = across_ref[:256, :], across_ref[256:, :]
        else:
            lanes = slice(0, 128)
            ah, al = across_ref[128:256, :], across_ref[384:, :]
        done = mm(vh[:, lanes], ah) + (mm(vl[:, lanes], ah) + mm(vh[:, lanes], al))
        here = slice(128 * j, 128 * j + 128)
        place = slice(8 * (j % 2), 8 * (j % 2) + 8)
        for band in range(4):
            part = done[4 * count * (band // 2) : 4 * count * (band // 2) + 4 * count]
            part = part[:, 128 * (band % 2) : 128 * (band % 2) + 128].reshape(4, count, 128)
            blended = dual_ref[band, four, :, here] + part
            blend_ref[band, four, :, here] = blended
            squares = jnp.sum(blended * blended, axis=0)
            for strip in range(count // 8):
                energy_ref[j // 2, 4 * band + first // 8 + strip, place, :] += squares[
                    8 * strip : 8 * strip + 8
                ]


def inner_kernel(
    sky_in,
    dual_in,
    down_in,
    across_in,
    blend_out,
    energy_out,
    sky_ref,
    dual_ref,
    down_ref,
    across_ref,
    blend_ref,
    energy_ref,
    in_sems,
    out_sems,
):
    fours = [slice(4 * k, 4 * k + 4) for k in range(4)]
    down = copy_in(down_in, down_ref, in_sems.at[0])
    sky, dual = [], []
    for k, four in enumerate(fours):
        sky.append(copy_in(sky_in.at[four], sky_ref.at[four], in_sems.at[2 + k]))
        if k == 0:
            across = copy_in(across_in, across_ref, in_sems.at[1])
        dual.append(copy_in(dual_in.at[:, four, 8:], dual_ref.at[:, four], in_sems.at[6 + k]))
    energy_ref[...] = jnp.zeros_like(energy_ref)
    down.wait()
    going = []
    for k, four in enumerate(fours):
        sky[k].wait()
        if k == 0:
            across.wait()
        dual[k].wait()
        pieces = [sky_ref[c] for c in range(4 * k, 4 * k + 4)]
        blend_group(pieces, four, 8, down_ref, across_ref, dual_ref, blend_ref, energy_ref)
        going.append(copy_in(blend_ref.at[:, four], blend_out.at[:4, four, 8:], out_sems.at[k]))
    going.append(copy_in(energy_ref, energy_out, out_sems.at[4]))
    for copy in going:
        copy.wait()


def outer_kernel(
    margins_ref,
    sky_in,
    rim_in,
    dual_in,
    down_in,
    across_in,
    energy_in,
    blend_in,
    blend_out,
    sent_out,
    sky_ref,
    rim_ref,
    dual_ref,
    down_ref,
    across_ref,
    blend_ref,
    energy_ref,
    in_sems,
    out_sems,
):
    margin = margins_ref[lax.axis_index("facet")]
    half = lax.axis_index("chan") % 2
    row = lax.broadcasted_iota(jnp.int32, (8, 512), 0)
    kept = row >= 8 - margin
    coming = [
        copy_in(source, target, in_sems.at[k])
        for k, (source, target) in enumerate(
            (
                (rim_in, rim_ref),
                (sky_in.at[:, :8], sky_ref),
                (down_in, down_ref),
                (across_in, across_ref),
                (energy_in, energy_ref),
                (dual_in.at[:, :, :8], dual_ref),
            )
        )
    ]
    for copy in coming:
        copy.wait()
    going = []
    for k in range(4):
        four = slice(4 * k, 4 * k + 4)
        pieces = []
        for c in range(4 * k, 4 * k + 4):
            pieces += [jnp.where(kept, rim_ref[c], 0.0), sky_ref[c]]
        blend_group(pieces, four, 0, down_ref, across_ref, dual_ref, blend_ref, energy_ref)
        going.append(copy_in(blend_ref.at[:, four], blend_out.at[:4, four, :8], out_sems.at[k]))
    going.append(copy_in(energy_ref.at[1 - half], sent_out, out_sems.at[4]))
    going.append(copy_in(energy_ref.at[half], blend_out.at[4, :, :16, :128], out_sems.at[5]))
    for copy in going:
        copy.wait()


def blend_inner(sky, dual):
    down, across = (jnp.asarray(t) for t in filter_tables(8, 32))
    hbm = pl.BlockSpec(memory_space=pl.ANY)
    return pl.pallas_call(
        inner_kernel,
        in_specs=[hbm] * 4,
        out_specs=(hbm, hbm),
        out_shape=(
            jax.ShapeDtypeStruct((ROOM, 16, 32, 512), f32),
            jax.ShapeDtypeStruct((2, 16, 16, 128), f32),
        ),
        scratch_shapes=[
            pltpu.VMEM(sky.shape, f32),
            pltpu.VMEM((4, 16, 24, 512), f32),
            pltpu.VMEM(down.shape, bf16),
            pltpu.VMEM(across.shape, bf16),
            pltpu.VMEM((4, 16, 24, 512), f32),
            pltpu.VMEM((2, 16, 16, 128), f32),
            pltpu.SemaphoreType.DMA((10,)),
            pltpu.SemaphoreType.DMA((5,)),
        ],
        compiler_params=params(60),
        cost_estimate=cost(2e9, 8 * MIB),
        name="blend_inner",
    )(sky, dual, down, across)


def blend_outer(margins, sky, rim, dual, energy, blended):
    down, across = (jnp.asarray(t) for t in filter_tables(0, 8))
    hbm = pl.BlockSpec(memory_space=pl.ANY)
    return pl.pallas_call(
        outer_kernel,
        in_specs=[pl.BlockSpec(memory_space=pltpu.SMEM)] + [hbm] * 7,
        out_specs=(hbm, hbm),
        out_shape=(
            jax.ShapeDtypeStruct(blended.shape, f32),
            jax.ShapeDtypeStruct((16, 16, 128), f32),
        ),
        input_output_aliases={7: 0},
        scratch_shapes=[
            pltpu.VMEM((16, 8, 512), f32),
            pltpu.VMEM((16, 8, 512), f32),
            pltpu.VMEM((4, 16, 8, 512), f32),
            pltpu.VMEM(down.shape, bf16),
            pltpu.VMEM(across.shape, bf16),
            pltpu.VMEM((4, 16, 8, 512), f32),
            pltpu.VMEM((2, 16, 16, 128), f32),
            pltpu.SemaphoreType.DMA((6,)),
            pltpu.SemaphoreType.DMA((6,)),
        ],
        compiler_params=params(60),
        cost_estimate=cost(1e9, 4 * MIB),
        name="blend_outer",
    )(margins, sky, rim, dual, down, across, energy, blended)


def degrid_tables(side):
    column = np.arange(side, dtype=np.int64)[None, :]
    kx = np.arange(KT, dtype=np.int64)[:, None]
    tile = np.arange(side // KT, dtype=np.int64)[:, None]
    inner = (kx * column % side) * (2.0 * np.pi / side)
    outer = (KT * tile * column % side) * (2.0 * np.pi / side)
    columns = np.concatenate([np.cos(inner), np.sin(inner), np.cos(outer), np.sin(outer)])
    ky, row = np.arange(16)[:, None], np.arange(32)[None, :]
    turn = ky * row * (2.0 * np.pi / side)
    whole = np.zeros((16, 4, 2, 2, 4, 32))
    for ch in range(4):
        whole[:, ch, 0, 0, ch, :] = np.cos(turn)
        whole[:, ch, 0, 1, ch, :] = np.sin(turn)
        whole[:, ch, 1, 0, ch, :] = -np.sin(turn)
        whole[:, ch, 1, 1, ch, :] = np.cos(turn)
    rows = np.concatenate(host_halves(whole.reshape(128, 256)))
    shift = np.arange(32)[:, None] * np.arange(32)[None, :] * (2.0 * np.pi / 32)
    shift = np.concatenate(host_halves(np.concatenate([np.cos(shift), np.sin(shift)])))
    turn = np.arange(16) * (2.0 * np.pi / 16)
    turn = np.stack([np.cos(turn), np.sin(turn)]).astype(np.float32)
    return columns.astype(np.float32), rows, shift, turn


def channel_at(place):
    b0, b3, b1, b2 = ((place >> k) & 1 for k in (3, 2, 1, 0))
    return b0 + 2 * b1 + 4 * b2 + 8 * b3


def degrid_kernel(
    tile_ref,
    turn_ref,
    sky_ref,
    shift_ref,
    column_ref,
    row_ref,
    weight_in,
    sent_out,
    mine_out,
    out_ref,
    xh_ref,
    xl_ref,
    table_ref,
    t_ref,
    u_ref,
    weight_ref,
    sem,
):
    coming = copy_in(weight_in, weight_ref, sem.at[0])
    facet = lax.axis_index("facet")
    inner_cos, inner_sin = column_ref[:KT, :], column_ref[KT : 2 * KT, :]
    block = lax.broadcasted_iota(jnp.int32, (8, 512), 1) // KT
    ty = jnp.zeros((8, 512), jnp.int32)
    for b in range(32):
        tile = tile_ref[0, b]
        ty = jnp.where(block == b, tile // 32, ty)
        outer_cos = column_ref[pl.ds(2 * KT + tile % 32, 1), :]
        outer_sin = column_ref[pl.ds(2 * KT + 32 + tile % 32, 1), :]
        rows = slice(KT * b, KT * b + KT)
        both = (
            inner_cos * outer_cos - inner_sin * outer_sin,
            inner_sin * outer_cos + inner_cos * outer_sin,
        )
        for k, values in enumerate(both):
            upper, lower = halves(values)
            table_ref[2 * k, rows, :] = upper
            table_ref[2 * k + 1, rows, :] = lower
    for place in range(16):
        xh, xl = halves(sky_ref[channel_at(place)])
        xh_ref[32 * place : 32 * place + 32, :] = xh
        xl_ref[32 * place : 32 * place + 32, :] = xl
    wanted = lax.broadcasted_iota(jnp.int32, (32, 512), 0) == ty[:1, :]
    phase = mm(shift_ref[...], wanted.astype(f32).astype(bf16))
    phase = (phase[:64] + phase[64:]).reshape(2, 32, 512)
    cos_h, cos_l, sin_h, sin_l = (table_ref[k] for k in range(4))
    row_h, row_l = row_ref[:128, :], row_ref[128:, :]
    for half in range(4):
        rows = slice(128 * half, 128 * half + 128)
        xh, xl = xh_ref[rows, :], xl_ref[rows, :]
        gc = mm_t(xh, cos_h) + (mm_t(xl, cos_h) + mm_t(xh, cos_l))
        gs = mm_t(xh, sin_h) + (mm_t(xl, sin_h) + mm_t(xh, sin_l))
        gc, gs = gc.reshape(4, 32, 512), gs.reshape(4, 32, 512)
        pc, ps = phase[0][None], phase[1][None]
        pre = (gc * pc - gs * ps).reshape(128, 512)
        pim = (-(gs * pc + gc * ps)).reshape(128, 512)
        both_h, both_l = halves(jnp.concatenate([pre, pim], axis=0))
        t_ref[half] = mm(row_h, both_h) + (mm(row_l, both_h) + mm(row_h, both_l))
    even = lax.broadcasted_iota(jnp.int32, (8, 128), 0) % 2 == 0
    coming.wait()
    for quarter in range(4):
        for four in range(4):
            for high in range(2):
                parts = []
                for low in range(8):
                    ky = 8 * high + low
                    part = t_ref[four, 8 * ky : 8 * ky + 8, 128 * quarter : 128 * quarter + 128]
                    other = jnp.where(even, pltpu.roll(part, 7, 0), -pltpu.roll(part, 1, 0))
                    spot = ky * facet % 16
                    parts.append(part * turn_ref[0, spot] + other * turn_ref[1, spot])
                for b, done in enumerate(swap_chunks(parts, 16)):
                    u_ref[32 * b + 8 * four : 32 * b + 8 * four + 8, 128 * high : 128 * high + 128] = done
        uh, ul = halves(u_ref[...])
        rows = slice(256 * quarter, 256 * quarter + 256)
        sums = []
        for part in range(2):
            weights = weight_ref[rows, 256 * part : 256 * part + 256]
            sums.append(mm_t(uh, weights) + mm_t(ul, weights))
        lane = lax.broadcasted_iota(jnp.int32, (32, 256), 1)
        row = lax.broadcasted_iota(jnp.int32, (32, 256), 0)
        first = jnp.zeros((32, 256), f32)
        second = jnp.zeros((32, 256), f32)
        for b in range(8):
            mine = lane // 32 == b
            first = jnp.where(mine, sums[0][32 * b : 32 * b + 32, :], first)
            second = jnp.where(mine, sums[1][32 * b : 32 * b + 32, :], second)
        other = jnp.where(row % 2 == 0, -pltpu.roll(second, 31, 0), pltpu.roll(second, 1, 0))
        out_ref[:, 256 * quarter : 256 * quarter + 256] = (first + other) * (1.0 / 512.0)
    core = facet % 2
    going = [
        copy_in(out_ref.at[pl.ds(pl.multiple_of(16 * which, 16), 16)], target, sem.at[k])
        for k, (which, target) in enumerate(((1 - core, sent_out), (core, mine_out)))
    ]
    for copy in going:
        copy.wait()


def degrid(sky, weights, tile_ids):
    columns, rows, shift, turn = (jnp.asarray(t) for t in degrid_tables(sky.shape[-1]))
    smem = pl.BlockSpec(memory_space=pltpu.SMEM)
    vmem = pl.BlockSpec(memory_space=pltpu.VMEM)
    hbm = pl.BlockSpec(memory_space=pl.ANY)
    return pl.pallas_call(
        degrid_kernel,
        in_specs=[smem, smem] + [vmem] * 4 + [hbm],
        out_specs=(hbm, hbm),
        out_shape=(jax.ShapeDtypeStruct((16, 1024), f32),) * 2,
        scratch_shapes=[
            pltpu.VMEM((32, 1024), f32),
            pltpu.VMEM((512, 512), bf16),
            pltpu.VMEM((512, 512), bf16),
            pltpu.VMEM((4, 512, 512), bf16),
            pltpu.VMEM((4, 128, 512), f32),
            pltpu.VMEM((256, 256), f32),
            pltpu.VMEM((1024, 512), bf16),
            pltpu.SemaphoreType.DMA((2,)),
        ],
        compiler_params=params(60),
        cost_estimate=cost(3e9, 6 * MIB),
        name="degrid",
    )(tile_ids, turn, sky, shift, columns, rows, weights)


def data_kernel(radius_ref, dual_ref, forward_ref, vis_ref, out_ref):
    vis = vis_ref[0]
    moved = dual_ref[0] + forward_ref[...]
    residual = 2.0 * moved - vis
    distance = jnp.sqrt(jnp.sum(residual * residual, keepdims=True) + 1e-06)
    radius = radius_ref[0] * math.sqrt(2.0 * vis.shape[1])
    out_ref[0] = moved - 0.5 * (vis + residual * jnp.minimum(1.0, radius / distance))


def data_step(data_dual, forward, visibilities, radius_scale):
    vmem = pl.BlockSpec(memory_space=pltpu.VMEM)
    return pl.pallas_call(
        data_kernel,
        in_specs=[pl.BlockSpec(memory_space=pltpu.SMEM)] + [vmem] * 3,
        out_specs=vmem,
        out_shape=jax.ShapeDtypeStruct(data_dual.shape, f32),
        compiler_params=params(16),
        cost_estimate=cost(1e5, 1e5),
        name="data_step",
    )(radius_scale, data_dual, forward, visibilities)


def trade(values, axis):
    return lax.all_to_all(values, axis, 0, 0, tiled=True)


def facet_pairs(bit):
    return [(i, i ^ (1 << bit)) for i in range(lax.axis_size("facet"))]


def halving_sum(values, bits):
    me = lax.axis_index("facet")
    for bit in bits:
        values = values.reshape(2, values.shape[0] // 2, values.shape[1])
        mine = (me >> bit) & 1
        sent = lax.dynamic_index_in_dim(values, 1 - mine, 0, keepdims=False)
        kept = lax.dynamic_index_in_dim(values, mine, 0, keepdims=False)
        values = kept + lax.ppermute(sent, "facet", facet_pairs(bit))
    return values


def per_device(
    sky_image,
    margins,
    wavelet_dual,
    sparsity_weights,
    lowrank_dual,
    kernel_weights,
    tile_index,
    data_dual,
    visibilities,
    radius_scale,
):
    facet_rows, image_side = sky_image.shape[1:]
    channels = lowrank_dual.shape[0]
    devices = lax.axis_size("facet")

    packed, rim = pack_sky(sky_image)
    packed, sky = lax.optimization_barrier((packed, sky_image))
    got = trade(packed, "chan").reshape(2048, 128)
    rim = lax.ppermute(rim, "facet", [(i, i + 1) for i in range(devices - 1)])
    blended, energy = blend_inner(sky, wavelet_dual)
    blended, sent = blend_outer(margins, sky, rim, wavelet_dual, energy, blended)
    sky, sent = lax.optimization_barrier((sky, sent))
    other = lax.ppermute(sent, "chan", [(i, i ^ 1) for i in range(lax.axis_size("chan"))])
    sent, mine = degrid(sky, kernel_weights.reshape(1024, 512), tile_index)
    seen = lax.ppermute(sent, "facet", facet_pairs(0))
    other, mine, seen = lax.optimization_barrier((other, mine, seen))

    dual = jnp.transpose(lowrank_dual, (1, 2, 0)).reshape(4, 8, 32, 256)
    y, part = gram_part(got, dual, blended, other)
    part, mine, seen = lax.optimization_barrier((part, mine, seen))
    forward = halving_sum(mine + seen, (3,))
    reduced, forward = lax.optimization_barrier((trade(part, "chan"), forward))
    forward = halving_sum(forward, (1, 2))
    data_next = data_step(data_dual, forward, visibilities, radius_scale)
    summed, far = sum_copies(reduced)
    total = trade(summed, "chan")
    wavelet_next, mixed = finish(
        total, far, sparsity_weights, blended, y.reshape(2 * ROOM, 1024, 256), facet_rows * image_side, channels
    )
    lowrank_next = jnp.transpose(mixed.reshape(32, 32, 256), (2, 0, 1))
    return (wavelet_next, lowrank_next, data_next)


def solution(mesh):
    in_specs = (
        P("chan", "facet", None),
        P(),
        P(None, "chan", "facet", None),
        P(None, "facet", None),
        P(None, "facet", "chan"),
        P("chan", None, None, None),
        P("chan", None),
        P(("chan", "facet"), None, None),
        P(("chan", "facet"), None, None),
        P(("chan", "facet")),
    )
    out_specs = (
        P(None, "chan", "facet", None),
        P(None, "facet", "chan"),
        P(("chan", "facet"), None, None),
    )
    return jax.shard_map(
        per_device, mesh=mesh, in_specs=in_specs, out_specs=out_specs, check_vma=False
    )
```

```python
import math

import jax
import jax.numpy as jnp
import ml_dtypes
import numpy as np
from jax import lax
from jax.experimental import pallas as pl
from jax.experimental.pallas import tpu as pltpu
from jax.sharding import PartitionSpec as P

NSTEP = 5
KT = 16
MIB = 1 << 20
ROOM = 24

low_taps = (
    -0.010597401784997278,
    0.032883011666982945,
    0.030841381835986965,
    -0.18703481171888114,
    -0.02798376941698385,
    0.6308807679295904,
    0.7148465705525415,
    0.23037781330885523,
)
high_taps = tuple(((-1.0) ** offset * low_taps[7 - offset] for offset in range(8)))
f32 = jnp.float32
bf16 = jnp.bfloat16


def params(mib):
    return pltpu.CompilerParams(vmem_limit_bytes=int(mib * MIB))


def cost(flops, nbytes):
    return pl.CostEstimate(flops=int(flops), bytes_accessed=int(nbytes), transcendentals=0)


def halves(values):
    upper = values.astype(bf16)
    return upper, (values - upper.astype(f32)).astype(bf16)


def host_halves(values):
    values = values.astype(np.float32)
    upper = values.astype(ml_dtypes.bfloat16)
    return upper, (values - upper.astype(np.float32)).astype(ml_dtypes.bfloat16)


def mm(a, b):
    return jnp.dot(a, b, preferred_element_type=f32)


def mm_t(a, b):
    return lax.dot_general(a, b, (((1,), (1,)), ((), ())), preferred_element_type=f32)


def mm3_right(a, bh, bl):
    ah, al = halves(a)
    return mm(ah, bh) + (mm(ah, bl) + mm(al, bh))


def swap_chunks(parts, width):
    count = len(parts)
    lane = lax.broadcasted_iota(jnp.int32, parts[0].shape, len(parts[0].shape) - 1)
    axis = len(parts[0].shape) - 1
    step = count // 2
    while step:
        span = step * width
        first = (lane // span) % 2 == 0
        out = list(parts)
        for a in range(count):
            if a & step:
                continue
            b = a | step
            out[a] = jnp.where(first, parts[a], pltpu.roll(parts[b], span, axis))
            out[b] = jnp.where(first, pltpu.roll(parts[a], 128 - span, axis), parts[b])
        parts = out
        step //= 2
    return parts


def pack_kernel(sky_in, packed_out, rim_out, sky_ref, packed_ref, in_sems, out_sems):
    fours = [slice(4 * k, 4 * k + 4) for k in range(4)]
    coming = [
        pltpu.make_async_copy(sky_in.at[four], sky_ref.at[four], in_sems.at[k])
        for k, four in enumerate(fours)
    ]
    going = [
        pltpu.make_async_copy(packed_ref.at[:, four], packed_out.at[:, four], out_sems.at[k])
        for k, four in enumerate(fours)
    ]
    going.append(pltpu.make_async_copy(sky_ref.at[:, 24:, :], rim_out, out_sems.at[4]))
    for copy in coming:
        copy.start()
    for k, four in enumerate(fours):
        coming[k].wait()
        for quarter in range(4):
            lanes = slice(128 * quarter, 128 * quarter + 128)
            parts = [sky_ref[four, 8 * j : 8 * j + 8, lanes] for j in range(4)]
            for s, done in enumerate(swap_chunks(parts, 32)):
                packed_ref[4 * quarter + s, four] = done
        going[k].start()
    going[4].start()
    for copy in going:
        copy.wait()


def pack_sky(sky):
    hbm = pl.BlockSpec(memory_space=pl.ANY)
    return pl.pallas_call(
        pack_kernel,
        in_specs=[hbm],
        out_specs=(hbm, hbm),
        out_shape=(
            jax.ShapeDtypeStruct((16, 16, 8, 128), f32),
            jax.ShapeDtypeStruct((16, 8, 512), f32),
        ),
        scratch_shapes=[
            pltpu.VMEM((16, 32, 512), f32),
            pltpu.VMEM((16, 16, 8, 128), f32),
            pltpu.SemaphoreType.DMA((4,)),
            pltpu.SemaphoreType.DMA((5,)),
        ],
        compiler_params=params(60),
        cost_estimate=cost(3e6, 2 * MIB),
        name="pack_sky",
    )(sky)


def turn_rows(block):
    row = lax.broadcasted_iota(jnp.int32, block.shape, 0)
    for bit in (1, 2, 4, 8):
        turned = pltpu.roll(block, 256 - bit, 1)
        block = jnp.where((row // bit) % 2 == 1, turned, block)
    return block


def gram_kernel(
    got_ref, dual_ref, blend_in, other_ref, y_out, part_out, y_ref, kept_ref, sum_ref, gram_ref, sems
):
    kept = copy_in(blend_in.at[4, :, :16, :128], kept_ref, sems.at[10])
    total = jnp.zeros((256, 256), f32)
    cross = jnp.zeros((256, 256), f32)
    held, copies = [], []
    for low in range(8):
        seen = got_ref[pl.ds(low, 256, stride=8), :].T
        right = dual_ref[:, low].reshape(128, 256) + 0.5 * seen
        rh, rl = halves(right)
        y_ref[0, :, low] = rh.reshape(4, 32, 256)
        y_ref[1, :, low] = rl.reshape(4, 32, 256)
        copies.append(pltpu.make_async_copy(y_ref.at[:, :, low], y_out.at[:2, :, low], sems.at[low]))
        copies[-1].start()
        held.append((rh, rl))
        if low % 4 == 3:
            rh = jnp.concatenate([upper for upper, _ in held], axis=0)
            rl = jnp.concatenate([lower for _, lower in held], axis=0)
            held = []
            lh = rh.T
            total = total + mm(lh, rh)
            cross = cross + mm(lh, rl)
    total = total + (cross + cross.T)
    kept.wait()
    sum_ref[...] = kept_ref[...] + other_ref[...]
    copies.append(copy_in(sum_ref, part_out.at[:, :16], sems.at[8]))
    row = lax.broadcasted_iota(jnp.int32, (128, 128), 0)
    lane = lax.broadcasted_iota(jnp.int32, (128, 128), 1)
    far = jnp.sum(jnp.where(row == lane, total[:128, 128:], 0.0), axis=0, keepdims=True)
    gram_ref[:, 16:, :] = jnp.broadcast_to(far[None], (16, 8, 128))
    for peer in range(16):
        turned = total[16 * peer : 16 * peer + 16, :]
        if peer:
            turned = pltpu.roll(turned, 256 - 16 * peer, 1)
        gram_ref[peer, :16, :] = turn_rows(turned)[:, :128]
    copies.append(pltpu.make_async_copy(gram_ref, part_out.at[:, 16:], sems.at[9]))
    copies[-1].start()
    for copy in copies:
        copy.wait()


def gram_part(got, dual, blended, other):
    vmem = pl.BlockSpec(memory_space=pltpu.VMEM)
    hbm = pl.BlockSpec(memory_space=pl.ANY)
    return pl.pallas_call(
        gram_kernel,
        in_specs=[vmem, vmem, hbm, vmem],
        out_specs=(hbm, hbm),
        out_shape=(
            jax.ShapeDtypeStruct((2 * ROOM, 4, 8, 32, 256), bf16),
            jax.ShapeDtypeStruct((16, 40, 128), f32),
        ),
        scratch_shapes=[
            pltpu.VMEM((2, 4, 8, 32, 256), bf16),
            pltpu.VMEM((16, 16, 128), f32),
            pltpu.VMEM((16, 16, 128), f32),
            pltpu.VMEM((16, 24, 128), f32),
            pltpu.SemaphoreType.DMA((11,)),
        ],
        compiler_params=params(40),
        cost_estimate=cost(4e8, 3 * MIB),
        name="gram_part",
    )(got, dual, blended, other)


def sum_kernel(got_ref, out_ref, far_ref):
    halves_of = [got_ref[0, :16], got_ref[1, :16]]
    gram = got_ref[0, 16:]
    for peer in range(1, 16):
        gram = gram + got_ref[peer, 16:]
        if peer > 1:
            halves_of[peer % 2] = halves_of[peer % 2] + got_ref[peer, :16]
    far_ref[...] = gram[16:]
    for peer in range(16):
        out_ref[peer, :16] = halves_of[0]
        out_ref[peer, 16:32] = halves_of[1]
        out_ref[peer, 32:] = gram[:16]


def sum_copies(got):
    return pl.pallas_call(
        sum_kernel,
        out_shape=(
            jax.ShapeDtypeStruct((16, 48, 128), f32),
            jax.ShapeDtypeStruct((8, 128), f32),
        ),
        compiler_params=params(16),
        cost_estimate=cost(1e6, MIB),
        name="sum_copies",
    )(got)


def finish_kernel(
    pixels,
    channels,
    got_ref,
    far_ref,
    weight_in,
    blend_in,
    y_in,
    wave_out,
    mixed_out,
    weight_ref,
    blend_ref,
    wave_ref,
    y_ref,
    mixed_ref,
    in_sems,
    out_sems,
):
    coming = [
        pltpu.make_async_copy(weight_in, weight_ref, in_sems.at[5]),
        pltpu.make_async_copy(y_in.at[:2], y_ref, in_sems.at[4]),
    ]
    arrived = [
        pltpu.make_async_copy(blend_in.at[band], blend_ref.at[band], in_sems.at[band])
        for band in range(4)
    ]
    for copy in coming + arrived:
        copy.start()
    going = []

    def wave(band):
        if band == 0:
            coming[0].wait()
        arrived[band].wait()
        for part in range(4):
            rows = slice(8 * part, 8 * part + 8)
            for q in range(4):
                lanes = slice(128 * q, 128 * q + 128)
                energy = got_ref[4 * band + part, 8 * q : 8 * q + 8, :]
                ratio = jnp.sqrt(energy * (1.0 / channels)) / weight_ref[band, rows, lanes]
                scale = 1.0 / jnp.maximum(1.0, ratio)
                wave_ref[band, :, rows, lanes] = blend_ref[band, :, rows, lanes] * scale[None]
        copy = pltpu.make_async_copy(wave_ref.at[band], wave_out.at[band], out_sems.at[band])
        copy.start()
        going.append(copy)

    size = 256
    rows = lax.broadcasted_iota(jnp.int32, (size, size), 0)
    cols = lax.broadcasted_iota(jnp.int32, (size, size), 1)
    blocks = []
    nothing = jnp.zeros((16, 128), f32)
    for peer in range(16):
        block = jnp.concatenate([got_ref[peer, 32:48, :], nothing], axis=1)
        blocks.append(pltpu.roll(block, 16 * peer, 1, stride=1, stride_axis=0))
    half = jnp.concatenate(blocks, axis=0)
    far = far_ref[:1, :]
    apart = (cols - rows) % 256
    gram = jnp.where(apart < 128, half, half.T)
    gram = jnp.where(apart == 128, jnp.concatenate([far, far], axis=1), gram)
    shifted = (rows == cols).astype(f32) + gram * (1.0 / pixels)
    frob = jnp.sqrt(jnp.sum(shifted * shifted, keepdims=True))

    def middle_of(product):
        return jnp.where(rows == cols, 1.5, 0.0) - 0.5 * product

    product = shifted / frob
    middle = middle_of(product)
    inverse = middle
    for turn in range(1, NSTEP):
        mh, ml = halves(middle)
        if turn == 1:
            first = mm3_right(product, mh, ml)
        else:
            both = mm3_right(jnp.concatenate([product, inverse], axis=0), mh, ml)
            first, inverse = both[:size], both[size:]
        if turn > 2:
            wave(2 * turn - 6)
            wave(2 * turn - 5)
        product = mm3_right(first, mh, ml)
        middle = middle_of(product)
    mh, ml = halves(middle)
    mh, ml = halves(mm3_right(inverse, mh, ml) * lax.rsqrt(frob))
    coming[1].wait()
    for block in range(4):
        span = pl.ds(256 * block, 256)
        yh = y_ref[0, span, :]
        mixed_ref[span, :] = mm(yh, mh) + (mm(yh, ml) + mm(y_ref[1, span, :], mh))
        copy = pltpu.make_async_copy(mixed_ref.at[span], mixed_out.at[span], out_sems.at[4 + block])
        copy.start()
        going.append(copy)
    for copy in going:
        copy.wait()


def finish(got, far, weights, blended, y, pixels, channels):
    shape = (4, 16, 32, 512)
    hbm = pl.BlockSpec(memory_space=pl.ANY)
    return pl.pallas_call(
        lambda *refs: finish_kernel(pixels, channels, *refs),
        in_specs=[pl.BlockSpec(memory_space=pltpu.VMEM)] * 2 + [hbm] * 3,
        out_specs=(hbm, hbm),
        out_shape=(
            jax.ShapeDtypeStruct(shape, f32),
            jax.ShapeDtypeStruct((1024, 256), f32),
        ),
        scratch_shapes=[
            pltpu.VMEM(weights.shape, f32),
            pltpu.VMEM(shape, f32),
            pltpu.VMEM(shape, f32),
            pltpu.VMEM((2, 1024, 256), bf16),
            pltpu.VMEM((1024, 256), f32),
            pltpu.SemaphoreType.DMA((6,)),
            pltpu.SemaphoreType.DMA((8,)),
        ],
        compiler_params=params(40),
        cost_estimate=cost(2e9, 8 * MIB),
        name="finish",
    )(got, far, weights, blended, y)


def filter_tables(first, last):
    both = (low_taps, high_taps)
    count = last - first
    down = np.zeros((2, 4, count, 4, count + 8))
    across = np.zeros((256, 2, 128))
    for which, taps in enumerate(both):
        for m, tap in enumerate(taps):
            for row in range(count):
                for ch in range(4):
                    down[which, ch, row, ch, 8 + row - m] = tap
            for col in range(128):
                across[128 + col - m, which, col] = 0.5 * tap
    down = np.stack(host_halves(down.reshape(8 * count, 4 * count + 32)))
    return down, np.concatenate(host_halves(across.reshape(256, 256)))


def copy_in(source, target, sem):
    copy = pltpu.make_async_copy(source, target, sem)
    copy.start()
    return copy


def blend_group(pieces, four, first, down_ref, across_ref, dual_ref, blend_ref, energy_ref):
    count = dual_ref.shape[2]
    eh, el = halves(jnp.concatenate(pieces, axis=0))
    dh, dl = down_ref[0], down_ref[1]
    filtered = mm(dh, eh) + (mm(dh, el) + mm(dl, eh))
    vh, vl = halves(filtered)
    for j in range(4):
        if j:
            lanes = slice(128 * j - 128, 128 * j + 128)
            ah, al = across_ref[:256, :], across_ref[256:, :]
        else:
            lanes = slice(0, 128)
            ah, al = across_ref[128:256, :], across_ref[384:, :]
        done = mm(vh[:, lanes], ah) + (mm(vl[:, lanes], ah) + mm(vh[:, lanes], al))
        here = slice(128 * j, 128 * j + 128)
        place = slice(8 * (j % 2), 8 * (j % 2) + 8)
        for band in range(4):
            part = done[4 * count * (band // 2) : 4 * count * (band // 2) + 4 * count]
            part = part[:, 128 * (band % 2) : 128 * (band % 2) + 128].reshape(4, count, 128)
            blended = dual_ref[band, four, :, here] + part
            blend_ref[band, four, :, here] = blended
            squares = jnp.sum(blended * blended, axis=0)
            for strip in range(count // 8):
                energy_ref[j // 2, 4 * band + first // 8 + strip, place, :] += squares[
                    8 * strip : 8 * strip + 8
                ]


def inner_kernel(
    sky_in,
    dual_in,
    down_in,
    across_in,
    blend_out,
    energy_out,
    sky_ref,
    dual_ref,
    down_ref,
    across_ref,
    blend_ref,
    energy_ref,
    in_sems,
    out_sems,
):
    fours = [slice(4 * k, 4 * k + 4) for k in range(4)]
    down = copy_in(down_in, down_ref, in_sems.at[0])
    sky, dual = [], []
    for k, four in enumerate(fours):
        sky.append(copy_in(sky_in.at[four], sky_ref.at[four], in_sems.at[2 + k]))
        if k == 0:
            across = copy_in(across_in, across_ref, in_sems.at[1])
        dual.append(copy_in(dual_in.at[:, four, 8:], dual_ref.at[:, four], in_sems.at[6 + k]))
    energy_ref[...] = jnp.zeros_like(energy_ref)
    down.wait()
    going = []
    for k, four in enumerate(fours):
        sky[k].wait()
        if k == 0:
            across.wait()
        dual[k].wait()
        pieces = [sky_ref[c] for c in range(4 * k, 4 * k + 4)]
        blend_group(pieces, four, 8, down_ref, across_ref, dual_ref, blend_ref, energy_ref)
        going.append(copy_in(blend_ref.at[:, four], blend_out.at[:4, four, 8:], out_sems.at[k]))
    going.append(copy_in(energy_ref, energy_out, out_sems.at[4]))
    for copy in going:
        copy.wait()


def outer_kernel(
    margins_ref,
    sky_in,
    rim_in,
    dual_in,
    down_in,
    across_in,
    energy_in,
    blend_in,
    blend_out,
    sent_out,
    sky_ref,
    rim_ref,
    dual_ref,
    down_ref,
    across_ref,
    blend_ref,
    energy_ref,
    in_sems,
    out_sems,
):
    margin = margins_ref[lax.axis_index("facet")]
    half = lax.axis_index("chan") % 2
    row = lax.broadcasted_iota(jnp.int32, (8, 512), 0)
    kept = row >= 8 - margin
    coming = [
        copy_in(source, target, in_sems.at[k])
        for k, (source, target) in enumerate(
            (
                (rim_in, rim_ref),
                (sky_in.at[:, :8], sky_ref),
                (down_in, down_ref),
                (across_in, across_ref),
                (energy_in, energy_ref),
                (dual_in.at[:, :, :8], dual_ref),
            )
        )
    ]
    for copy in coming:
        copy.wait()
    going = []
    for k in range(4):
        four = slice(4 * k, 4 * k + 4)
        pieces = []
        for c in range(4 * k, 4 * k + 4):
            pieces += [jnp.where(kept, rim_ref[c], 0.0), sky_ref[c]]
        blend_group(pieces, four, 0, down_ref, across_ref, dual_ref, blend_ref, energy_ref)
        going.append(copy_in(blend_ref.at[:, four], blend_out.at[:4, four, :8], out_sems.at[k]))
    going.append(copy_in(energy_ref.at[1 - half], sent_out, out_sems.at[4]))
    going.append(copy_in(energy_ref.at[half], blend_out.at[4, :, :16, :128], out_sems.at[5]))
    for copy in going:
        copy.wait()


def blend_inner(sky, dual):
    down, across = (jnp.asarray(t) for t in filter_tables(8, 32))
    hbm = pl.BlockSpec(memory_space=pl.ANY)
    return pl.pallas_call(
        inner_kernel,
        in_specs=[hbm] * 4,
        out_specs=(hbm, hbm),
        out_shape=(
            jax.ShapeDtypeStruct((ROOM, 16, 32, 512), f32),
            jax.ShapeDtypeStruct((2, 16, 16, 128), f32),
        ),
        scratch_shapes=[
            pltpu.VMEM(sky.shape, f32),
            pltpu.VMEM((4, 16, 24, 512), f32),
            pltpu.VMEM(down.shape, bf16),
            pltpu.VMEM(across.shape, bf16),
            pltpu.VMEM((4, 16, 24, 512), f32),
            pltpu.VMEM((2, 16, 16, 128), f32),
            pltpu.SemaphoreType.DMA((10,)),
            pltpu.SemaphoreType.DMA((5,)),
        ],
        compiler_params=params(60),
        cost_estimate=cost(2e9, 8 * MIB),
        name="blend_inner",
    )(sky, dual, down, across)


def blend_outer(margins, sky, rim, dual, energy, blended):
    down, across = (jnp.asarray(t) for t in filter_tables(0, 8))
    hbm = pl.BlockSpec(memory_space=pl.ANY)
    return pl.pallas_call(
        outer_kernel,
        in_specs=[pl.BlockSpec(memory_space=pltpu.SMEM)] + [hbm] * 7,
        out_specs=(hbm, hbm),
        out_shape=(
            jax.ShapeDtypeStruct(blended.shape, f32),
            jax.ShapeDtypeStruct((16, 16, 128), f32),
        ),
        input_output_aliases={7: 0},
        scratch_shapes=[
            pltpu.VMEM((16, 8, 512), f32),
            pltpu.VMEM((16, 8, 512), f32),
            pltpu.VMEM((4, 16, 8, 512), f32),
            pltpu.VMEM(down.shape, bf16),
            pltpu.VMEM(across.shape, bf16),
            pltpu.VMEM((4, 16, 8, 512), f32),
            pltpu.VMEM((2, 16, 16, 128), f32),
            pltpu.SemaphoreType.DMA((6,)),
            pltpu.SemaphoreType.DMA((6,)),
        ],
        compiler_params=params(60),
        cost_estimate=cost(1e9, 4 * MIB),
        name="blend_outer",
    )(margins, sky, rim, dual, down, across, energy, blended)


def degrid_tables(side):
    column = np.arange(side, dtype=np.int64)[None, :]
    kx = np.arange(KT, dtype=np.int64)[:, None]
    tile = np.arange(side // KT, dtype=np.int64)[:, None]
    inner = (kx * column % side) * (2.0 * np.pi / side)
    outer = (KT * tile * column % side) * (2.0 * np.pi / side)
    columns = np.concatenate([np.cos(inner), np.sin(inner), np.cos(outer), np.sin(outer)])
    ky, row = np.arange(16)[:, None], np.arange(32)[None, :]
    turn = ky * row * (2.0 * np.pi / side)
    whole = np.zeros((16, 4, 2, 2, 4, 32))
    for ch in range(4):
        whole[:, ch, 0, 0, ch, :] = np.cos(turn)
        whole[:, ch, 0, 1, ch, :] = np.sin(turn)
        whole[:, ch, 1, 0, ch, :] = -np.sin(turn)
        whole[:, ch, 1, 1, ch, :] = np.cos(turn)
    rows = np.concatenate(host_halves(whole.reshape(128, 256)))
    shift = np.arange(32)[:, None] * np.arange(32)[None, :] * (2.0 * np.pi / 32)
    shift = np.concatenate(host_halves(np.concatenate([np.cos(shift), np.sin(shift)])))
    turn = np.arange(16) * (2.0 * np.pi / 16)
    turn = np.stack([np.cos(turn), np.sin(turn)]).astype(np.float32)
    return columns.astype(np.float32), rows, shift, turn


def channel_at(place):
    b0, b3, b1, b2 = ((place >> k) & 1 for k in (3, 2, 1, 0))
    return b0 + 2 * b1 + 4 * b2 + 8 * b3


def degrid_kernel(
    tile_ref,
    turn_ref,
    sky_ref,
    shift_ref,
    column_ref,
    row_ref,
    weight_in,
    sent_out,
    mine_out,
    out_ref,
    xh_ref,
    xl_ref,
    table_ref,
    t_ref,
    u_ref,
    weight_ref,
    sem,
):
    coming = copy_in(weight_in, weight_ref, sem.at[0])
    facet = lax.axis_index("facet")
    inner_cos, inner_sin = column_ref[:KT, :], column_ref[KT : 2 * KT, :]
    block = lax.broadcasted_iota(jnp.int32, (8, 512), 1) // KT
    ty = jnp.zeros((8, 512), jnp.int32)
    for b in range(32):
        tile = tile_ref[0, b]
        ty = jnp.where(block == b, tile // 32, ty)
        outer_cos = column_ref[pl.ds(2 * KT + tile % 32, 1), :]
        outer_sin = column_ref[pl.ds(2 * KT + 32 + tile % 32, 1), :]
        rows = slice(KT * b, KT * b + KT)
        both = (
            inner_cos * outer_cos - inner_sin * outer_sin,
            inner_sin * outer_cos + inner_cos * outer_sin,
        )
        for k, values in enumerate(both):
            upper, lower = halves(values)
            table_ref[2 * k, rows, :] = upper
            table_ref[2 * k + 1, rows, :] = lower
    for place in range(16):
        xh, xl = halves(sky_ref[channel_at(place)])
        xh_ref[32 * place : 32 * place + 32, :] = xh
        xl_ref[32 * place : 32 * place + 32, :] = xl
    wanted = lax.broadcasted_iota(jnp.int32, (32, 512), 0) == ty[:1, :]
    phase = mm(shift_ref[...], wanted.astype(f32).astype(bf16))
    phase = (phase[:64] + phase[64:]).reshape(2, 32, 512)
    cos_h, cos_l, sin_h, sin_l = (table_ref[k] for k in range(4))
    row_h, row_l = row_ref[:128, :], row_ref[128:, :]
    for half in range(4):
        rows = slice(128 * half, 128 * half + 128)
        xh, xl = xh_ref[rows, :], xl_ref[rows, :]
        gc = mm_t(xh, cos_h) + (mm_t(xl, cos_h) + mm_t(xh, cos_l))
        gs = mm_t(xh, sin_h) + (mm_t(xl, sin_h) + mm_t(xh, sin_l))
        gc, gs = gc.reshape(4, 32, 512), gs.reshape(4, 32, 512)
        pc, ps = phase[0][None], phase[1][None]
        pre = (gc * pc - gs * ps).reshape(128, 512)
        pim = (-(gs * pc + gc * ps)).reshape(128, 512)
        both_h, both_l = halves(jnp.concatenate([pre, pim], axis=0))
        t_ref[half] = mm(row_h, both_h) + (mm(row_l, both_h) + mm(row_h, both_l))
    even = lax.broadcasted_iota(jnp.int32, (8, 128), 0) % 2 == 0
    coming.wait()
    for quarter in range(4):
        for four in range(4):
            for high in range(2):
                parts = []
                for low in range(8):
                    ky = 8 * high + low
                    part = t_ref[four, 8 * ky : 8 * ky + 8, 128 * quarter : 128 * quarter + 128]
                    other = jnp.where(even, pltpu.roll(part, 7, 0), -pltpu.roll(part, 1, 0))
                    spot = ky * facet % 16
                    parts.append(part * turn_ref[0, spot] + other * turn_ref[1, spot])
                for b, done in enumerate(swap_chunks(parts, 16)):
                    u_ref[32 * b + 8 * four : 32 * b + 8 * four + 8, 128 * high : 128 * high + 128] = done
        uh, ul = halves(u_ref[...])
        rows = slice(256 * quarter, 256 * quarter + 256)
        sums = []
        for part in range(2):
            weights = weight_ref[rows, 256 * part : 256 * part + 256]
            sums.append(mm_t(uh, weights) + mm_t(ul, weights))
        lane = lax.broadcasted_iota(jnp.int32, (32, 256), 1)
        row = lax.broadcasted_iota(jnp.int32, (32, 256), 0)
        first = jnp.zeros((32, 256), f32)
        second = jnp.zeros((32, 256), f32)
        for b in range(8):
            mine = lane // 32 == b
            first = jnp.where(mine, sums[0][32 * b : 32 * b + 32, :], first)
            second = jnp.where(mine, sums[1][32 * b : 32 * b + 32, :], second)
        other = jnp.where(row % 2 == 0, -pltpu.roll(second, 31, 0), pltpu.roll(second, 1, 0))
        out_ref[:, 256 * quarter : 256 * quarter + 256] = (first + other) * (1.0 / 512.0)
    core = facet % 2
    going = [
        copy_in(out_ref.at[pl.ds(pl.multiple_of(16 * which, 16), 16)], target, sem.at[k])
        for k, (which, target) in enumerate(((1 - core, sent_out), (core, mine_out)))
    ]
    for copy in going:
        copy.wait()


def degrid(sky, weights, tile_ids):
    columns, rows, shift, turn = (jnp.asarray(t) for t in degrid_tables(sky.shape[-1]))
    smem = pl.BlockSpec(memory_space=pltpu.SMEM)
    vmem = pl.BlockSpec(memory_space=pltpu.VMEM)
    hbm = pl.BlockSpec(memory_space=pl.ANY)
    return pl.pallas_call(
        degrid_kernel,
        in_specs=[smem, smem] + [vmem] * 4 + [hbm],
        out_specs=(hbm, hbm),
        out_shape=(jax.ShapeDtypeStruct((16, 1024), f32),) * 2,
        scratch_shapes=[
            pltpu.VMEM((32, 1024), f32),
            pltpu.VMEM((512, 512), bf16),
            pltpu.VMEM((512, 512), bf16),
            pltpu.VMEM((4, 512, 512), bf16),
            pltpu.VMEM((4, 128, 512), f32),
            pltpu.VMEM((256, 256), f32),
            pltpu.VMEM((1024, 512), bf16),
            pltpu.SemaphoreType.DMA((2,)),
        ],
        compiler_params=params(60),
        cost_estimate=cost(3e9, 6 * MIB),
        name="degrid",
    )(tile_ids, turn, sky, shift, columns, rows, weights)


def data_kernel(radius_ref, dual_ref, forward_ref, vis_ref, out_ref):
    vis = vis_ref[0]
    moved = dual_ref[0] + forward_ref[...]
    residual = 2.0 * moved - vis
    distance = jnp.sqrt(jnp.sum(residual * residual, keepdims=True) + 1e-06)
    radius = radius_ref[0] * math.sqrt(2.0 * vis.shape[1])
    out_ref[0] = moved - 0.5 * (vis + residual * jnp.minimum(1.0, radius / distance))


def data_step(data_dual, forward, visibilities, radius_scale):
    vmem = pl.BlockSpec(memory_space=pltpu.VMEM)
    return pl.pallas_call(
        data_kernel,
        in_specs=[pl.BlockSpec(memory_space=pltpu.SMEM)] + [vmem] * 3,
        out_specs=vmem,
        out_shape=jax.ShapeDtypeStruct(data_dual.shape, f32),
        compiler_params=params(16),
        cost_estimate=cost(1e5, 1e5),
        name="data_step",
    )(radius_scale, data_dual, forward, visibilities)


def trade(values, axis):
    return lax.all_to_all(values, axis, 0, 0, tiled=True)


def facet_pairs(bit):
    return [(i, i ^ (1 << bit)) for i in range(lax.axis_size("facet"))]


def halving_sum(values, bits):
    me = lax.axis_index("facet")
    for bit in bits:
        values = values.reshape(2, values.shape[0] // 2, values.shape[1])
        mine = (me >> bit) & 1
        sent = lax.dynamic_index_in_dim(values, 1 - mine, 0, keepdims=False)
        kept = lax.dynamic_index_in_dim(values, mine, 0, keepdims=False)
        values = kept + lax.ppermute(sent, "facet", facet_pairs(bit))
    return values


def per_device(
    sky_image,
    margins,
    wavelet_dual,
    sparsity_weights,
    lowrank_dual,
    kernel_weights,
    tile_index,
    data_dual,
    visibilities,
    radius_scale,
):
    facet_rows, image_side = sky_image.shape[1:]
    channels = lowrank_dual.shape[0]
    devices = lax.axis_size("facet")

    packed, rim = pack_sky(sky_image)
    packed, sky = lax.optimization_barrier((packed, sky_image))
    got = trade(packed, "chan").reshape(2048, 128)
    rim = lax.ppermute(rim, "facet", [(i, i + 1) for i in range(devices - 1)])
    blended, energy = blend_inner(sky, wavelet_dual)
    blended, sent = blend_outer(margins, sky, rim, wavelet_dual, energy, blended)
    sky, sent = lax.optimization_barrier((sky, sent))
    other = lax.ppermute(sent, "chan", [(i, i ^ 1) for i in range(lax.axis_size("chan"))])
    sent, mine = degrid(sky, kernel_weights.reshape(1024, 512), tile_index)
    seen = lax.ppermute(sent, "facet", facet_pairs(0))
    other, mine, seen = lax.optimization_barrier((other, mine, seen))

    dual = jnp.transpose(lowrank_dual, (1, 2, 0)).reshape(4, 8, 32, 256)
    y, part = gram_part(got, dual, blended, other)
    part, mine, seen = lax.optimization_barrier((part, mine, seen))
    forward = halving_sum(mine + seen, (3,))
    reduced, forward = lax.optimization_barrier((trade(part, "chan"), forward))
    forward = halving_sum(forward, (1, 2))
    data_next = data_step(data_dual, forward, visibilities, radius_scale)
    summed, far = sum_copies(reduced)
    total = trade(summed, "chan")
    wavelet_next, mixed = finish(
        total, far, sparsity_weights, blended, y.reshape(2 * ROOM, 1024, 256), facet_rows * image_side, channels
    )
    lowrank_next = jnp.transpose(mixed.reshape(32, 32, 256), (2, 0, 1))
    return (wavelet_next, lowrank_next, data_next)


def solution(mesh):
    in_specs = (
        P("chan", "facet", None),
        P(),
        P(None, "chan", "facet", None),
        P(None, "facet", None),
        P(None, "facet", "chan"),
        P("chan", None, None, None),
        P("chan", None),
        P(("chan", "facet"), None, None),
        P(("chan", "facet"), None, None),
        P(("chan", "facet")),
    )
    out_specs = (
        P(None, "chan", "facet", None),
        P(None, "facet", "chan"),
        P(("chan", "facet"), None, None),
    )
    return jax.shard_map(
        per_device, mesh=mesh, in_specs=in_specs, out_specs=out_specs, check_vma=False
    )
```
